512 devices in a mesh: grp: 32 (over z, y_hi), col: 16 (over x, y_lo, core).
Axes of the slice: x: 4, y: 4 (y_hi: 2, y_lo: 2; y = y_hi * 2 + y_lo), z: 16, core: 2. Of those that a mesh axis runs over, the one named last changes fastest.
Arguments:
- window_rows: bfloat16 [122880, 1024], P('grp', 'col'), may hold values from -0.0234375 to 0.0234375
- secular: bfloat16 [122880, 4096], P('grp', 'col'), may hold values from -6 to 6
- source: int32 [122880], P('grp'), may hold values from 0 to 122879, as said below
- kept_count: int32 [1], replicated, may hold values from 61440 to 122879
Outputs:
- merged: bfloat16 [2, 1024, 4096], P(None, 'grp', 'col')
The draws below stay inside these ranges and needn't reach their ends.
Inputs may be any that keep to these rules, and one draw needn't show every extreme that they name: source is a permutation of 0 to 122879; for j in block b of 3840 indices, source[j] lies in block b or in block b + 16 (b < 16) or b - 16 (b >= 16).
All inputs are finite; a program needn't handle non-finite values.
Results may differ from the reference program's by a relative error of at most 0.0011.
Values may be sent and summed in bfloat16 or wider, within the bound.
No kernel may reach another device: no remote copies, remote signals or barrier semaphores. Data moves between devices by JAX's collectives and lax.ppermute only.
A program may use at most 64 MiB of HBM per device.

```python
import jax
import jax.numpy as jnp
from jax import lax

N = 122880
RH = 1024
KS = 4096
BLK = 3840
PAIRS = 16


def draw_source(key, part):
    key = jax.random.fold_in(key, 7)
    counts = jax.random.randint(jax.random.fold_in(key, 1), (PAIRS,), 0, BLK + 1).astype(jnp.int32)
    chosen = jax.random.permutation(jax.random.fold_in(key, 2), PAIRS)
    counts = counts.at[chosen[0]].set(BLK).at[chosen[1]].set(0)
    positions = jnp.arange(BLK, dtype=jnp.int32)

    def one_pair(index, count):
        pair_key = jax.random.fold_in(jax.random.fold_in(key, 3), index)
        order_a = jax.random.permutation(jax.random.fold_in(pair_key, 1), BLK).astype(jnp.int32)
        order_b = jax.random.permutation(jax.random.fold_in(pair_key, 2), BLK).astype(jnp.int32)
        shuffle_a = jax.random.permutation(jax.random.fold_in(pair_key, 3), BLK).astype(jnp.int32)
        shuffle_b = jax.random.permutation(jax.random.fold_in(pair_key, 4), BLK).astype(jnp.int32)
        base_a = index * BLK
        base_b = (index + PAIRS) * BLK
        crossing = positions < count
        list_a = jnp.where(crossing, base_b + order_b, base_a + order_a)
        list_b = jnp.where(crossing, base_a + order_a, base_b + order_b)
        return jnp.concatenate([list_a[shuffle_a], list_b[shuffle_b]]).astype(jnp.int32)
    paired = jax.vmap(one_pair)(jnp.arange(PAIRS, dtype=jnp.int32), counts)
    first = paired[:, :BLK].reshape(-1)
    second = paired[:, BLK:].reshape(-1)
    return jnp.concatenate([first, second]).astype(jnp.int32)


def level_of(key, extent, split, low, largest):
    def one(dim, shards_of):
        draws = jax.random.uniform(jax.random.fold_in(jax.random.fold_in(key, 6), dim), (shards_of,), jnp.float32, low / len(split), largest / len(split))
        return jnp.repeat(jnp.exp(draws), extent[dim] // shards_of).reshape((-1,) + (1,) * (len(extent) - dim - 1))

    loudness = one(*split[0])
    for cut in split[1:]:
        loudness = loudness * one(*cut)
    return loudness


def normal_values(key, extent, deviation, most, cuts=(), held_as=jnp.bfloat16):
    values = jax.random.normal(key, extent, jnp.float32) * deviation
    if len(cuts) > 0:
        values = level_of(key, extent, cuts, -0.22, 0.18) * values
    return jnp.clip(values, min=-most, max=most).astype(held_as)


def setup_inputs(seed: int = 0) -> dict:
    key_list = jax.random.split(jax.random.key(seed), 5)
    return {
        "window_rows": normal_values(key_list[0], (N, RH), (N // 2) ** -0.5, 0.0234375, ((0, 32), (1, 16))),
        "secular": normal_values(key_list[1], (N, KS), 1.0, 6.0, ((0, 32), (1, 16))),
        "source": draw_source(jax.random.fold_in(key_list[4], 71), 0),
        "kept_count": jax.random.randint(key_list[3], (1,), N // 2, N).astype(jnp.int32),
    }


def reference(window_rows, secular, source, kept_count):
    limit = kept_count[0]
    valid = source < limit
    half = N // 2
    width = min(KS, 512)

    def one_block(index):
        columns = lax.dynamic_slice_in_dim(secular, index * width, width, 1)
        picked = jnp.where(valid[:, None], columns[source], jnp.zeros((), jnp.bfloat16))
        upper = jnp.dot(window_rows[:half].T, picked[:half], preferred_element_type=jnp.float32)
        lower = jnp.dot(window_rows[half:].T, picked[half:], preferred_element_type=jnp.float32)
        return jnp.stack([upper, lower])

    blocks = lax.map(one_block, jnp.arange(KS // width, dtype=jnp.int32))
    return blocks.transpose(1, 2, 0, 3).reshape(2, RH, KS).astype(jnp.bfloat16)
```

```python
import functools

import jax
import jax.numpy as jnp
from jax import lax
from jax.experimental import pallas as pl
from jax.experimental.pallas import tpu as pltpu
from jax.sharding import PartitionSpec as P

LANES = 128
UNROLL = 16
K_TILE = 768


def scatter_kernel(place_ref, w_ref, own_ref, cross_ref, flag_ref, rows, spread):
    width, blk = w_ref.shape
    tiles = blk // LANES
    ones = jnp.ones((LANES - width, LANES), jnp.float32)

    def load(i, carry):
        at = pl.multiple_of(i * LANES, LANES)
        part = w_ref[:, pl.ds(at, LANES)].astype(jnp.float32)
        rows[pl.ds(at, LANES), :] = jnp.concatenate([part, ones], axis=0).T
        spread[pl.ds(at, LANES), :] = jnp.zeros((LANES, LANES), jnp.float32)
        spread[pl.ds(blk + at, LANES), :] = jnp.zeros((LANES, LANES), jnp.float32)
        return carry

    lax.fori_loop(0, tiles, load, 0)

    def move(i, carry):
        for u in range(UNROLL):
            j = i * UNROLL + u
            spread[pl.ds(place_ref[j], 1), :] = rows[pl.ds(j, 1), :]
        return carry

    lax.fori_loop(0, blk // UNROLL, move, 0)

    def store(i, carry):
        at = pl.multiple_of(i * LANES, LANES)
        own = spread[pl.ds(at, LANES), :]
        own_ref[:, pl.ds(at, LANES)] = own.T[:width].astype(jnp.bfloat16)
        cross = spread[pl.ds(blk + at, LANES), :]
        cross_ref[:, pl.ds(at, LANES)] = cross.T[:width].astype(jnp.bfloat16)
        mark = own[:, width:]
        flag_ref[pl.ds(at, LANES), :] = jnp.concatenate([mark, mark], axis=1)
        return carry

    lax.fori_loop(0, tiles, store, 0)


def scatter_rows(place, w_t):
    width, blk = w_t.shape
    return pl.pallas_call(
        scatter_kernel,
        out_shape=[
            jax.ShapeDtypeStruct((width, blk), jnp.bfloat16),
            jax.ShapeDtypeStruct((width, blk), jnp.bfloat16),
            jax.ShapeDtypeStruct((blk, LANES), jnp.float32),
        ],
        in_specs=[pl.BlockSpec(memory_space=pltpu.SMEM), pl.BlockSpec(memory_space=pltpu.VMEM)],
        out_specs=[pl.BlockSpec(memory_space=pltpu.VMEM)] * 3,
        scratch_shapes=[pltpu.VMEM((blk, LANES), jnp.float32), pltpu.VMEM((2 * blk, LANES), jnp.float32)],
        compiler_params=pltpu.CompilerParams(vmem_limit_bytes=32 * 2**20),
    )(place, w_t)


def halves_kernel(info_ref, flag_ref, own_ref, other_ref, out_ref):
    tile, cols = own_ref.shape
    row = lax.broadcasted_iota(jnp.int32, (tile, LANES), 0) + pl.program_id(0) * tile
    mark = flag_ref[...]
    alive = row < info_ref[1]
    mine = alive & (mark > 0.5)
    theirs = alive & (mark < 0.5)
    lower = info_ref[0] > 0
    in_half = (
        jnp.where(lower, theirs.astype(jnp.float32), mine.astype(jnp.float32)),
        jnp.where(lower, mine.astype(jnp.float32), theirs.astype(jnp.float32)),
    )
    for c, ref in enumerate((own_ref, other_ref)):
        for h in range(2):
            for v in range(cols // LANES):
                values = ref[:, v * LANES : (v + 1) * LANES].astype(jnp.float32)
                at = (c * 2 + h) * cols + v * LANES
                out_ref[:, at : at + LANES] = jnp.where(in_half[h] > 0.5, values, 0.0).astype(jnp.bfloat16)


def split_halves(info, flag, own, other):
    blk, cols = own.shape
    return pl.pallas_call(
        halves_kernel,
        grid=(blk // K_TILE,),
        out_shape=jax.ShapeDtypeStruct((blk, 4 * cols), jnp.bfloat16),
        in_specs=[
            pl.BlockSpec(memory_space=pltpu.SMEM),
            pl.BlockSpec((K_TILE, LANES), lambda i: (i, 0)),
            pl.BlockSpec((K_TILE, cols), lambda i: (i, 0)),
            pl.BlockSpec((K_TILE, cols), lambda i: (i, 0)),
        ],
        out_specs=pl.BlockSpec((K_TILE, 4 * cols), lambda i: (i, 0)),
        compiler_params=pltpu.CompilerParams(vmem_limit_bytes=32 * 2**20),
    )(info, flag, own, other)


def product_kernel(slot_ref, *refs):
    pieces, s_ref, out_ref, total = refs[:-3], refs[-3], refs[-2], refs[-1]
    step = pl.program_id(0)
    rows = pieces[0].shape[0]
    lhs = jnp.concatenate([ref[...] for ref in pieces], axis=0)
    term = jnp.dot(lhs, s_ref[...], preferred_element_type=jnp.float32)

    @pl.when(step == 0)
    def _():
        total[...] = term

    @pl.when(step > 0)
    def _():
        total[...] += term

    @pl.when(step == pl.num_programs(0) - 1)
    def _():
        for i in range(len(pieces)):
            out_ref[slot_ref[i]] = total[i * rows : (i + 1) * rows, :]


def product(slots, pieces, s_both):
    rows, blk = pieces[0].shape
    cols = s_both.shape[1]
    count = len(pieces)
    return pl.pallas_call(
        product_kernel,
        grid=(blk // K_TILE,),
        out_shape=jax.ShapeDtypeStruct((count, rows, cols), jnp.float32),
        in_specs=[pl.BlockSpec(memory_space=pltpu.SMEM)]
        + [pl.BlockSpec((rows, K_TILE), lambda i: (0, i))] * count
        + [pl.BlockSpec((K_TILE, cols), lambda i: (i, 0))],
        out_specs=pl.BlockSpec((count, rows, cols), lambda i: (0, 0, 0)),
        scratch_shapes=[pltpu.VMEM((count * rows, cols), jnp.float32)],
        compiler_params=pltpu.CompilerParams(vmem_limit_bytes=48 * 2**20),
    )(slots, *pieces, s_both)


def col_move(value, target):
    pairs = []
    for c in range(16):
        x, y, core = c // 4, c // 2 % 2, c % 2
        tx, ty, tcore = target(x, y, core)
        pairs.append((c, tx % 4 * 4 + ty * 2 + tcore))
    return lax.ppermute(value, "col", pairs)


def slice_move(value, target):
    pairs = []
    for g in range(32):
        for c in range(16):
            to = target(g // 2, g % 2, c)
            if to is not None:
                pairs.append((g * 16 + c, (to[0] % 16 * 2 + to[1]) * 16 + to[2]))
    return lax.ppermute(value, ("grp", "col"), pairs)


def exchange(step, z, y_hi, c):
    even = (c - z) % 2 == 0
    return (z + 1 if even == (step % 2 == 1) else z - 1, y_hi, c)


ORDER_EVEN = (7, 6, 4, 2, 0, 1, 3, 5)
ORDER_ODD = (7, 5, 3, 1, 0, 2, 4, 6)


def per_device(window_rows, secular, source, kept_count):
    blk = secular.shape[0]
    g = lax.axis_index("grp")
    c = lax.axis_index("col")
    z, y_hi = g // 2, g % 2
    x, y_lo, core = c // 4, c // 2 % 2, c % 2
    odd = (core + z) % 2
    own_base = g * blk
    partner_base = jnp.bitwise_xor(g, 16) * blk

    other = col_move(secular, lambda x, y, k: (x, y, 1 - k))
    inside = (source >= own_base) & (source < own_base + blk)
    place = jnp.where(inside, source - own_base, blk + source - partner_base)
    own_part, cross_part, flag = scatter_rows(place, window_rows.T)
    arrived = lax.ppermute(cross_part, "grp", [(i, i ^ 16) for i in range(32)])
    info = jnp.stack([g // 16, kept_count[0] - own_base]).astype(jnp.int32)
    s_both = split_halves(info, flag, secular, other)

    here = own_part + arrived
    pieces = {(0, 0): here}
    for d in (1, 3, 2):
        pieces[d, 0] = col_move(here, lambda x, y, k, d=d: (x - d, y, k))
    pieces[0, 1] = col_move(here, lambda x, y, k: (x, 1 - y, k))
    pieces[2, 1] = col_move(pieces[0, 1], lambda x, y, k: (x - 2, y, k))
    for d in (1, 3):
        pieces[d, 1] = col_move(pieces[d, 0], lambda x, y, k: (x, 1 - y, k))

    places = list(pieces)
    targets = jnp.stack([(x + dx) % 4 * 4 + jnp.bitwise_xor(y_lo, dy) * 2 + core for dx, dy in places])
    above = (targets - z - odd) % 16 // 2
    orders = jnp.where(odd == 1, jnp.array(ORDER_ODD, jnp.int32), jnp.array(ORDER_EVEN, jnp.int32))
    slots = orders[above].astype(jnp.int32)
    terms = product(slots, [pieces[p] for p in places], s_both)

    moving = terms[0]
    for step in range(1, 8):
        moving = terms[step] + slice_move(moving, functools.partial(exchange, step))
    half_cols = moving.shape[1] // 2
    mine, theirs = moving[:, :half_cols], moving[:, half_cols:]
    is_odd = odd == 1

    def last(z, y_hi, c):
        return (z + 1, y_hi, c) if (c - z) % 2 else (z, y_hi, c ^ 1)

    def last_other(z, y_hi, c):
        return (z + 1, y_hi, c ^ 1) if (c - z) % 2 else None

    first_in = slice_move(jnp.where(is_odd, mine, theirs), last)
    second_in = slice_move(theirs, last_other)
    summed = jnp.where(is_odd, second_in, mine) + first_in
    rows = summed.shape[0] // 2
    low, high = summed[:rows], summed[rows:]
    is_high = y_hi == 1
    across = lax.ppermute(jnp.where(is_high, low, high), "grp", [(i, i ^ 1) for i in range(32)])
    final = (jnp.where(is_high, high, low) + across).astype(jnp.bfloat16)
    return final.reshape(rows, 2, half_cols // 2).transpose(1, 0, 2)


def solution(mesh):
    return jax.shard_map(
        per_device,
        mesh=mesh,
        in_specs=(P("grp", "col"), P("grp", "col"), P("grp"), P()),
        out_specs=P(None, "grp", "col"),
        check_vma=False,
    )
```

```python
import functools

import jax
import jax.numpy as jnp
from jax import lax
from jax.experimental import pallas as pl
from jax.experimental.pallas import tpu as pltpu
from jax.sharding import PartitionSpec as P

LANES = 128
UNROLL = 32
K_TILE = 768
CHUNKS = 2
PLACES = ((0, 0), (1, 0), (3, 0), (2, 0), (0, 1), (2, 1), (1, 1), (3, 1))


def scatter_kernel(place_ref, w_ref, *refs):
    outs, flag_ref, rows, spread = refs[:-3], refs[-3], refs[-2], refs[-1]
    width, blk = w_ref.shape
    part_rows = width // CHUNKS
    ones = jnp.ones((LANES - width, LANES), jnp.float32)
    spread[...] = jnp.zeros_like(spread)
    for at in range(0, blk, LANES):
        part = w_ref[:, at : at + LANES].astype(jnp.float32)
        rows[at : at + LANES, :] = jnp.concatenate([part, ones], axis=0).T

    def move(i, carry):
        for u in range(UNROLL):
            j = i * UNROLL + u
            spread[pl.ds(place_ref[j], 1), :] = rows[pl.ds(j, 1), :]
        return carry

    lax.fori_loop(0, blk // UNROLL, move, 0)
    for side in range(2):
        for at in range(0, blk, LANES):
            block = spread[side * blk + at : side * blk + at + LANES, :]
            turned = block.T[:width].astype(jnp.bfloat16)
            for h in range(CHUNKS):
                outs[side * CHUNKS + h][:, at : at + LANES] = turned[h * part_rows : (h + 1) * part_rows]
            if side == 0:
                mark = block[:, width:]
                flag_ref[at : at + LANES, :] = jnp.concatenate([mark, mark], axis=1).astype(jnp.bfloat16)


def scatter_rows(place, w_t):
    width, blk = w_t.shape
    return pl.pallas_call(
        scatter_kernel,
        out_shape=[jax.ShapeDtypeStruct((width // CHUNKS, blk), jnp.bfloat16)] * (2 * CHUNKS)
        + [jax.ShapeDtypeStruct((blk, LANES), jnp.bfloat16)],
        in_specs=[pl.BlockSpec(memory_space=pltpu.SMEM), pl.BlockSpec(memory_space=pltpu.VMEM)],
        out_specs=[pl.BlockSpec(memory_space=pltpu.VMEM)] * (2 * CHUNKS + 1),
        scratch_shapes=[pltpu.VMEM((blk, LANES), jnp.float32), pltpu.VMEM((2 * blk, LANES), jnp.float32)],
        compiler_params=pltpu.CompilerParams(vmem_limit_bytes=16 * 2**20),
    )(place, w_t)


def halves_kernel(kept_ref, flag_ref, own_ref, other_ref, out_ref, done_ref):
    tile, cols = own_ref.shape
    g = lax.axis_index("grp")
    base = (g * pl.num_programs(0) + pl.program_id(0)) * tile
    row = lax.broadcasted_iota(jnp.int32, (tile, LANES), 0) + base
    done_ref[...] = jnp.zeros_like(done_ref)
    mark = flag_ref[...].astype(jnp.float32)
    alive = row < kept_ref[0]
    mine = alive & (mark > 0.5)
    theirs = alive & (mark < 0.5)
    lower = g >= 16
    in_half = (
        jnp.where(lower, theirs.astype(jnp.float32), mine.astype(jnp.float32)),
        jnp.where(lower, mine.astype(jnp.float32), theirs.astype(jnp.float32)),
    )
    for c, ref in enumerate((own_ref, other_ref)):
        for h in range(2):
            for v in range(cols // LANES):
                values = ref[:, v * LANES : (v + 1) * LANES].astype(jnp.float32)
                at = (c * 2 + h) * cols + v * LANES
                out_ref[:, at : at + LANES] = jnp.where(in_half[h] > 0.5, values, 0.0).astype(jnp.bfloat16)


def split_halves(kept, flag, own, other):
    blk, cols = own.shape
    return pl.pallas_call(
        halves_kernel,
        grid=(blk // K_TILE,),
        out_shape=[
            jax.ShapeDtypeStruct((blk, 4 * cols), jnp.bfloat16),
            jax.ShapeDtypeStruct((8, LANES), jnp.float32),
        ],
        in_specs=[
            pl.BlockSpec(memory_space=pltpu.SMEM),
            pl.BlockSpec((K_TILE, LANES), lambda i: (i, 0)),
            pl.BlockSpec((K_TILE, cols), lambda i: (i, 0)),
            pl.BlockSpec((K_TILE, cols), lambda i: (i, 0)),
        ],
        out_specs=[pl.BlockSpec((K_TILE, 4 * cols), lambda i: (i, 0)), pl.BlockSpec((8, LANES), lambda i: (0, 0))],
        compiler_params=pltpu.CompilerParams(vmem_limit_bytes=12 * 2**20),
    )(kept, flag, own, other)


def slot_of(z, x, y_lo, core, dx, dy):
    odd = (core + z) % 2
    target = (x + dx) % 4 * 4 + (y_lo + dy) % 2 * 2 + core
    above = (target + 16 - z - odd) % 16 // 2
    even_slot = jnp.where(above > 4, 2 * above - 9, jnp.minimum(8 - 2 * above, 7))
    odd_slot = jnp.where(above > 4, 2 * above - 8, jnp.maximum(7 - 2 * above, 0))
    return jnp.where(odd == 1, odd_slot, even_slot)


def product_kernel(*refs):
    pieces, s_ref, out_ref, total = refs[:-3], refs[-3], refs[-2], refs[-1]
    z, c = lax.axis_index("grp") // 2, lax.axis_index("col")
    step = pl.program_id(0)
    rows = pieces[0].shape[0]
    lhs = jnp.concatenate([ref[...] for ref in pieces], axis=0)
    term = jnp.dot(lhs, s_ref[...], preferred_element_type=jnp.float32)

    @pl.when(step == 0)
    def _():
        total[...] = term

    @pl.when(step > 0)
    def _():
        total[...] += term

    @pl.when(step == pl.num_programs(0) - 1)
    def _():
        for i in range(len(pieces)):
            slot = slot_of(z, c // 4, c // 2 % 2, c % 2, *PLACES[i])
            out_ref[slot] = total[i * rows : (i + 1) * rows, :]


def product(pieces, s_both):
    rows, blk = pieces[0].shape
    cols = s_both.shape[1]
    count = len(pieces)
    return pl.pallas_call(
        product_kernel,
        grid=(blk // K_TILE,),
        out_shape=jax.ShapeDtypeStruct((count, rows, cols), jnp.float32),
        in_specs=[pl.BlockSpec((rows, K_TILE), lambda i: (0, i))] * count
        + [pl.BlockSpec((K_TILE, cols), lambda i: (i, 0))],
        out_specs=pl.BlockSpec((count, rows, cols), lambda i: (0, 0, 0)),
        scratch_shapes=[pltpu.VMEM((count * rows, cols), jnp.float32)],
        compiler_params=pltpu.CompilerParams(vmem_limit_bytes=16 * 2**20),
    )(*pieces, s_both)


def col_move(value, target):
    pairs = []
    for c in range(16):
        x, y, core = c // 4, c // 2 % 2, c % 2
        tx, ty, tcore = target(x, y, core)
        pairs.append((c, tx % 4 * 4 + ty * 2 + tcore))
    return lax.ppermute(value, "col", pairs)


def slice_move(value, target):
    pairs = []
    for g in range(32):
        for c in range(16):
            to = target(g // 2, g % 2, c)
            if to is not None:
                pairs.append((g * 16 + c, (to[0] % 16 * 2 + to[1]) * 16 + to[2]))
    return lax.ppermute(value, ("grp", "col"), pairs)


def exchange(step, z, y_hi, c):
    even = (c - z) % 2 == 0
    return (z + 1 if even == (step % 2 == 1) else z - 1, y_hi, c)


def combine_kernel(count, *refs):
    own_ref, arrived_ref = refs[0], refs[1]
    outs = refs[len(refs) - count :]
    outs[0][...] = own_ref[...] + arrived_ref[...]
    if count == 2:
        outs[1][...] = refs[2][...]


def combine(own, arrived, following, after):
    count = 1 if following is None else 2
    arrays = [own, arrived] + ([] if following is None else [following])
    whole = pl.BlockSpec(memory_space=pltpu.VMEM)
    return pl.pallas_call(
        functools.partial(combine_kernel, count),
        out_shape=[jax.ShapeDtypeStruct(own.shape, own.dtype)] * count,
        in_specs=[whole] * len(arrays) + [pl.BlockSpec(memory_space=pl.ANY)],
        out_specs=[whole] * count,
        compiler_params=pltpu.CompilerParams(vmem_limit_bytes=4 * 2**20),
    )(*arrays, after)


def gather_col(here):
    pieces = {(0, 0): here}
    for d in (1, 3, 2):
        pieces[d, 0] = col_move(here, lambda x, y, k, d=d: (x - d, y, k))
    pieces[0, 1] = col_move(here, lambda x, y, k: (x, 1 - y, k))
    pieces[2, 1] = col_move(pieces[0, 1], lambda x, y, k: (x - 2, y, k))
    for d in (1, 3):
        pieces[d, 1] = col_move(pieces[d, 0], lambda x, y, k: (x, 1 - y, k))
    return pieces


def last(z, y_hi, c):
    return (z + 1, y_hi, c) if (c - z) % 2 else (z, y_hi, c ^ 1)


def last_other(z, y_hi, c):
    return (z + 1, y_hi, c ^ 1) if (c - z) % 2 else None


def per_device(window_rows, secular, source, kept_count):
    blk = secular.shape[0]
    g = lax.axis_index("grp")
    c = lax.axis_index("col")
    z, y_hi = g // 2, g % 2
    is_odd = (c + z) % 2 == 1
    is_high = y_hi == 1
    own_base = g * blk
    partner_base = jnp.bitwise_xor(g, 16) * blk

    other = col_move(secular, lambda x, y, k: (x, y, 1 - k))
    inside = (source >= own_base) & (source < own_base + blk)
    place = jnp.where(inside, source - own_base, blk + source - partner_base)
    *parts, flag = scatter_rows(place, window_rows.T)
    own_parts, cross_parts = parts[:CHUNKS], parts[CHUNKS:]
    s_both, masked = split_halves(kept_count, flag, secular, other)

    sums = []
    leaving, after = cross_parts[0], masked
    for h in range(CHUNKS):
        arrived = lax.ppermute(leaving, "grp", [(i, i ^ 16) for i in range(32)])
        here, *next_leaving = combine(own_parts[h], arrived, cross_parts[h + 1] if h + 1 < CHUNKS else None, after)
        if next_leaving:
            leaving = next_leaving[0]
        pieces = gather_col(here)
        terms = product([pieces[p] for p in PLACES], s_both)
        after = pieces[3, 1]
        moving = terms[0]
        for step in range(1, 8):
            moving = terms[step] + slice_move(moving, functools.partial(exchange, step))
        half_cols = moving.shape[1] // 2
        mine, theirs = moving[:, :half_cols], moving[:, half_cols:]
        first_in = slice_move(jnp.where(is_odd, mine, theirs), last)
        second_in = slice_move(theirs, last_other)
        sums.append(jnp.where(is_odd, second_in, mine) + first_in)

    low, high = sums
    across = lax.ppermute(jnp.where(is_high, low, high), "grp", [(i, i ^ 1) for i in range(32)])
    final = (jnp.where(is_high, high, low) + across).astype(jnp.bfloat16)
    return final.reshape(final.shape[0], 2, -1).transpose(1, 0, 2)


def solution(mesh):
    return jax.shard_map(
        per_device,
        mesh=mesh,
        in_specs=(P("grp", "col"), P("grp", "col"), P("grp"), P()),
        out_specs=P(None, "grp", "col"),
        check_vma=False,
    )
```

```python
import functools

import jax
import jax.numpy as jnp
from jax import lax
from jax.experimental import pallas as pl
from jax.experimental.pallas import tpu as pltpu
from jax.sharding import PartitionSpec as P

LANES = 128
UNROLL = 32
K_TILE = 768
CHUNKS = 1
PLACES = ((0, 0), (1, 0), (3, 0), (2, 0), (0, 1), (2, 1), (1, 1), (3, 1))


def scatter_kernel(place_ref, w_ref, *refs):
    outs, flag_ref, rows, spread = refs[:-3], refs[-3], refs[-2], refs[-1]
    width, blk = w_ref.shape
    part_rows = width // CHUNKS
    ones = jnp.ones((LANES - width, LANES), jnp.float32)
    spread[...] = jnp.zeros_like(spread)
    for at in range(0, blk, LANES):
        part = w_ref[:, at : at + LANES].astype(jnp.float32)
        rows[at : at + LANES, :] = jnp.concatenate([part, ones], axis=0).T

    def move(i, carry):
        for u in range(UNROLL):
            j = i * UNROLL + u
            spread[pl.ds(place_ref[j], 1), :] = rows[pl.ds(j, 1), :]
        return carry

    lax.fori_loop(0, blk // UNROLL, move, 0)
    for side in range(2):
        for at in range(0, blk, LANES):
            block = spread[side * blk + at : side * blk + at + LANES, :]
            turned = block.T[:width].astype(jnp.bfloat16)
            for h in range(CHUNKS):
                outs[side * CHUNKS + h][:, at : at + LANES] = turned[h * part_rows : (h + 1) * part_rows]
            if side == 0:
                mark = block[:, width:]
                flag_ref[at : at + LANES, :] = jnp.concatenate([mark, mark], axis=1).astype(jnp.bfloat16)


def scatter_rows(place, w_t):
    width, blk = w_t.shape
    return pl.pallas_call(
        scatter_kernel,
        out_shape=[jax.ShapeDtypeStruct((width // CHUNKS, blk), jnp.bfloat16)] * (2 * CHUNKS)
        + [jax.ShapeDtypeStruct((blk, LANES), jnp.bfloat16)],
        in_specs=[pl.BlockSpec(memory_space=pltpu.SMEM), pl.BlockSpec(memory_space=pltpu.VMEM)],
        out_specs=[pl.BlockSpec(memory_space=pltpu.VMEM)] * (2 * CHUNKS + 1),
        scratch_shapes=[pltpu.VMEM((blk, LANES), jnp.float32), pltpu.VMEM((2 * blk, LANES), jnp.float32)],
        compiler_params=pltpu.CompilerParams(vmem_limit_bytes=16 * 2**20),
    )(place, w_t)


def halves_kernel(kept_ref, flag_ref, own_ref, other_ref, out_ref, done_ref):
    tile, cols = own_ref.shape
    g = lax.axis_index("grp")
    base = (g * pl.num_programs(0) + pl.program_id(0)) * tile
    row = lax.broadcasted_iota(jnp.int32, (tile, LANES), 0) + base
    done_ref[...] = jnp.zeros_like(done_ref)
    mark = flag_ref[...].astype(jnp.float32)
    alive = row < kept_ref[0]
    mine = alive & (mark > 0.5)
    theirs = alive & (mark < 0.5)
    lower = g >= 16
    in_half = (
        jnp.where(lower, theirs.astype(jnp.float32), mine.astype(jnp.float32)),
        jnp.where(lower, mine.astype(jnp.float32), theirs.astype(jnp.float32)),
    )
    for c, ref in enumerate((own_ref, other_ref)):
        for h in range(2):
            for v in range(cols // LANES):
                values = ref[:, v * LANES : (v + 1) * LANES].astype(jnp.float32)
                at = (c * 2 + h) * cols + v * LANES
                out_ref[:, at : at + LANES] = jnp.where(in_half[h] > 0.5, values, 0.0).astype(jnp.bfloat16)


def split_halves(kept, flag, own, other):
    blk, cols = own.shape
    return pl.pallas_call(
        halves_kernel,
        grid=(blk // K_TILE,),
        out_shape=[
            jax.ShapeDtypeStruct((blk, 4 * cols), jnp.bfloat16),
            jax.ShapeDtypeStruct((8, LANES), jnp.float32),
        ],
        in_specs=[
            pl.BlockSpec(memory_space=pltpu.SMEM),
            pl.BlockSpec((K_TILE, LANES), lambda i: (i, 0)),
            pl.BlockSpec((K_TILE, cols), lambda i: (i, 0)),
            pl.BlockSpec((K_TILE, cols), lambda i: (i, 0)),
        ],
        out_specs=[pl.BlockSpec((K_TILE, 4 * cols), lambda i: (i, 0)), pl.BlockSpec((8, LANES), lambda i: (0, 0))],
        compiler_params=pltpu.CompilerParams(vmem_limit_bytes=12 * 2**20),
    )(kept, flag, own, other)


def slot_of(z, x, y_lo, core, dx, dy):
    odd = (core + z) % 2
    target = (x + dx) % 4 * 4 + (y_lo + dy) % 2 * 2 + core
    above = (target + 16 - z - odd) % 16 // 2
    even_slot = jnp.where(above > 4, 2 * above - 9, jnp.minimum(8 - 2 * above, 7))
    odd_slot = jnp.where(above > 4, 2 * above - 8, jnp.maximum(7 - 2 * above, 0))
    return jnp.where(odd == 1, odd_slot, even_slot)


def product_kernel(*refs):
    pieces, s_ref, out_ref, total = refs[:-3], refs[-3], refs[-2], refs[-1]
    z, c = lax.axis_index("grp") // 2, lax.axis_index("col")
    step = pl.program_id(0)
    rows = out_ref.shape[1]
    lhs = jnp.concatenate([ref[...] for ref in pieces], axis=0)
    term = jnp.dot(lhs, s_ref[...], preferred_element_type=jnp.float32)

    @pl.when(step == 0)
    def _():
        total[...] = term

    @pl.when(step > 0)
    def _():
        total[...] += term

    @pl.when(step == pl.num_programs(0) - 1)
    def _():
        for i, place in enumerate(PLACES):
            slot = slot_of(z, c // 4, c // 2 % 2, c % 2, *place)
            out_ref[slot] = total[i * rows : (i + 1) * rows, :]


def product(pieces, s_both, half):
    rows, blk = pieces[0].shape
    cols = s_both.shape[1] // 2
    block_rows = rows * len(pieces) // len(PLACES)
    return pl.pallas_call(
        product_kernel,
        grid=(blk // K_TILE,),
        out_shape=jax.ShapeDtypeStruct((len(PLACES), block_rows, cols), jnp.float32),
        in_specs=[pl.BlockSpec((rows, K_TILE), lambda i: (0, i))] * len(pieces)
        + [pl.BlockSpec((K_TILE, cols), lambda i: (i, half))],
        out_specs=pl.BlockSpec((len(PLACES), block_rows, cols), lambda i: (0, 0, 0)),
        scratch_shapes=[pltpu.VMEM((len(PLACES) * block_rows, cols), jnp.float32)],
        compiler_params=pltpu.CompilerParams(vmem_limit_bytes=12 * 2**20),
    )(*pieces, s_both)


def col_move(value, target):
    pairs = []
    for c in range(16):
        x, y, core = c // 4, c // 2 % 2, c % 2
        tx, ty, tcore = target(x, y, core)
        pairs.append((c, tx % 4 * 4 + ty * 2 + tcore))
    return lax.ppermute(value, "col", pairs)


def slice_move(value, target):
    pairs = []
    for g in range(32):
        for c in range(16):
            to = target(g // 2, g % 2, c)
            if to is not None:
                pairs.append((g * 16 + c, (to[0] % 16 * 2 + to[1]) * 16 + to[2]))
    return lax.ppermute(value, ("grp", "col"), pairs)


def exchange(step, z, y_hi, c):
    even = (c - z) % 2 == 0
    return (z + 1 if even == (step % 2 == 1) else z - 1, y_hi, c)


def combine_kernel(count, *refs):
    own_ref, arrived_ref = refs[0], refs[1]
    outs = refs[len(refs) - count :]
    outs[0][...] = own_ref[...] + arrived_ref[...]
    if count == 2:
        outs[1][...] = refs[2][...]


def combine(own, arrived, following, after):
    count = 1 if following is None else 2
    arrays = [own, arrived] + ([] if following is None else [following])
    whole = pl.BlockSpec(memory_space=pltpu.VMEM)
    return pl.pallas_call(
        functools.partial(combine_kernel, count),
        out_shape=[jax.ShapeDtypeStruct(own.shape, own.dtype)] * count,
        in_specs=[whole] * len(arrays) + [pl.BlockSpec(memory_space=pl.ANY)],
        out_specs=[whole] * count,
        compiler_params=pltpu.CompilerParams(vmem_limit_bytes=4 * 2**20),
    )(*arrays, after)


def gather_col(here):
    pieces = {(0, 0): here}
    for d in (1, 3, 2):
        pieces[d, 0] = col_move(here, lambda x, y, k, d=d: (x - d, y, k))
    pieces[0, 1] = col_move(here, lambda x, y, k: (x, 1 - y, k))
    pieces[2, 1] = col_move(pieces[0, 1], lambda x, y, k: (x - 2, y, k))
    for d in (1, 3):
        pieces[d, 1] = col_move(pieces[d, 0], lambda x, y, k: (x, 1 - y, k))
    return pieces


def per_device(window_rows, secular, source, kept_count):
    blk = secular.shape[0]
    g = lax.axis_index("grp")
    c = lax.axis_index("col")
    z, y_hi = g // 2, g % 2
    is_odd = (c + z) % 2 == 1
    own_base = g * blk
    partner_base = jnp.bitwise_xor(g, 16) * blk

    other = col_move(secular, lambda x, y, k: (x, y, 1 - k))
    inside = (source >= own_base) & (source < own_base + blk)
    place = jnp.where(inside, source - own_base, blk + source - partner_base)
    *parts, flag = scatter_rows(place, window_rows.T)
    own_parts, cross_parts = parts[:CHUNKS], parts[CHUNKS:]
    s_both, masked = split_halves(kept_count, flag, secular, other)

    pieces = []
    leaving, after = cross_parts[0], masked
    for h in range(CHUNKS):
        arrived = lax.ppermute(leaving, "grp", [(i, i ^ 16) for i in range(32)])
        here, *next_leaving = combine(own_parts[h], arrived, cross_parts[h + 1] if h + 1 < CHUNKS else None, after)
        if next_leaving:
            leaving = next_leaving[0]
        gathered = gather_col(here)
        pieces.append(gathered)
        after = gathered[3, 1]
    pieces = [gathered[p] for p in PLACES for gathered in pieces]

    s_both = pltpu.with_memory_space_constraint(s_both, pltpu.HBM)
    terms = [product(pieces, s_both, half) for half in range(2)]
    moving = [term[0] for term in terms]
    for step in range(1, 8):
        for half in range(2):
            moving[half] = terms[half][step] + slice_move(moving[half], functools.partial(exchange, step))

    mine, theirs = moving
    rows = mine.shape[0] // 2

    def part(value, y):
        return jnp.where(y == 1, value[rows:], value[:rows])

    def odd_or_even(when_odd, when_even):
        def target(z, y_hi, c):
            is_odd = (c - z) % 2
            flips = when_odd if is_odd else when_even
            return None if flips is None else (z + is_odd, y_hi ^ flips[0], c ^ flips[1])

        return target

    mine_here, mine_across = part(mine, y_hi), part(mine, 1 - y_hi)
    theirs_here, theirs_across = part(theirs, y_hi), part(theirs, 1 - y_hi)
    total = slice_move(theirs_across, odd_or_even((1, 1), None))
    total += slice_move(jnp.where(is_odd, mine_here, theirs_here), odd_or_even((0, 0), (0, 1)))
    total += slice_move(jnp.where(is_odd, mine_across, theirs_across), odd_or_even((1, 0), (1, 1)))
    total += slice_move(jnp.where(is_odd, theirs_here, mine_across), odd_or_even((0, 1), (1, 0)))
    final = jnp.where(is_odd, total, total + mine_here).astype(jnp.bfloat16)
    return final.reshape(rows, 2, -1).transpose(1, 0, 2)


def solution(mesh):
    return jax.shard_map(
        per_device,
        mesh=mesh,
        in_specs=(P("grp", "col"), P("grp", "col"), P("grp"), P()),
        out_specs=P(None, "grp", "col"),
        check_vma=False,
    )
```

```python
import functools

import jax
import jax.numpy as jnp
from jax import lax
from jax.experimental import pallas as pl
from jax.experimental.pallas import tpu as pltpu
from jax.sharding import PartitionSpec as P

LANES = 128
UNROLL = 32
K_TILE = 768
CHUNKS = 2
PLACES = ((0, 0), (1, 0), (3, 0), (2, 0), (0, 1), (2, 1), (1, 1), (3, 1))


def scatter_kernel(place_ref, w_ref, *refs):
    outs, flag_ref, rows, spread = refs[:-3], refs[-3], refs[-2], refs[-1]
    width, blk = w_ref.shape
    part_rows = width // CHUNKS
    ones = jnp.ones((LANES - width, LANES), jnp.float32)
    spread[...] = jnp.zeros_like(spread)
    for at in range(0, blk, LANES):
        part = w_ref[:, at : at + LANES].astype(jnp.float32)
        rows[at : at + LANES, :] = jnp.concatenate([part, ones], axis=0).T

    def move(i, carry):
        for u in range(UNROLL):
            j = i * UNROLL + u
            spread[pl.ds(place_ref[j], 1), :] = rows[pl.ds(j, 1), :]
        return carry

    lax.fori_loop(0, blk // UNROLL, move, 0)
    for side in range(2):
        for at in range(0, blk, LANES):
            block = spread[side * blk + at : side * blk + at + LANES, :]
            turned = block.T[:width].astype(jnp.bfloat16)
            for h in range(CHUNKS):
                outs[side * CHUNKS + h][:, at : at + LANES] = turned[h * part_rows : (h + 1) * part_rows]
            if side == 0:
                mark = block[:, width:]
                flag_ref[at : at + LANES, :] = jnp.concatenate([mark, mark], axis=1).astype(jnp.bfloat16)


def scatter_rows(place, w_t):
    width, blk = w_t.shape
    return pl.pallas_call(
        scatter_kernel,
        out_shape=[jax.ShapeDtypeStruct((width // CHUNKS, blk), jnp.bfloat16)] * (2 * CHUNKS)
        + [jax.ShapeDtypeStruct((blk, LANES), jnp.bfloat16)],
        in_specs=[pl.BlockSpec(memory_space=pltpu.SMEM), pl.BlockSpec(memory_space=pltpu.VMEM)],
        out_specs=[pl.BlockSpec(memory_space=pltpu.VMEM)] * (2 * CHUNKS + 1),
        scratch_shapes=[pltpu.VMEM((blk, LANES), jnp.float32), pltpu.VMEM((2 * blk, LANES), jnp.float32)],
        compiler_params=pltpu.CompilerParams(vmem_limit_bytes=16 * 2**20),
    )(place, w_t)


def halves_kernel(kept_ref, flag_ref, own_ref, other_ref, out_ref, done_ref):
    tile, cols = own_ref.shape
    g = lax.axis_index("grp")
    base = (g * pl.num_programs(0) + pl.program_id(0)) * tile
    row = lax.broadcasted_iota(jnp.int32, (tile, LANES), 0) + base
    done_ref[...] = jnp.zeros_like(done_ref)
    mark = flag_ref[...].astype(jnp.float32)
    alive = row < kept_ref[0]
    mine = alive & (mark > 0.5)
    theirs = alive & (mark < 0.5)
    lower = g >= 16
    in_half = (
        jnp.where(lower, theirs.astype(jnp.float32), mine.astype(jnp.float32)),
        jnp.where(lower, mine.astype(jnp.float32), theirs.astype(jnp.float32)),
    )
    for c, ref in enumerate((own_ref, other_ref)):
        for h in range(2):
            for v in range(cols // LANES):
                values = ref[:, v * LANES : (v + 1) * LANES].astype(jnp.float32)
                at = (c * 2 + h) * cols + v * LANES
                out_ref[:, at : at + LANES] = jnp.where(in_half[h] > 0.5, values, 0.0).astype(jnp.bfloat16)


def split_halves(kept, flag, own, other):
    blk, cols = own.shape
    return pl.pallas_call(
        halves_kernel,
        grid=(blk // K_TILE,),
        out_shape=[
            jax.ShapeDtypeStruct((blk, 4 * cols), jnp.bfloat16),
            jax.ShapeDtypeStruct((8, LANES), jnp.float32),
        ],
        in_specs=[
            pl.BlockSpec(memory_space=pltpu.SMEM),
            pl.BlockSpec((K_TILE, LANES), lambda i: (i, 0)),
            pl.BlockSpec((K_TILE, cols), lambda i: (i, 0)),
            pl.BlockSpec((K_TILE, cols), lambda i: (i, 0)),
        ],
        out_specs=[pl.BlockSpec((K_TILE, 4 * cols), lambda i: (i, 0)), pl.BlockSpec((8, LANES), lambda i: (0, 0))],
        compiler_params=pltpu.CompilerParams(vmem_limit_bytes=12 * 2**20),
    )(kept, flag, own, other)


def slot_of(z, x, y_lo, core, dx, dy):
    odd = (core + z) % 2
    target = (x + dx) % 4 * 4 + (y_lo + dy) % 2 * 2 + core
    above = (target + 16 - z - odd) % 16 // 2
    even_slot = jnp.where(above > 4, 2 * above - 9, jnp.minimum(8 - 2 * above, 7))
    odd_slot = jnp.where(above > 4, 2 * above - 8, jnp.maximum(7 - 2 * above, 0))
    return jnp.where(odd == 1, odd_slot, even_slot)


def product_kernel(*refs):
    count = len(refs) - 6
    pieces, s_hbm, outs = refs[:count], refs[count], refs[count + 1 : count + 3]
    total, s_ref, sems = refs[count + 3 :]
    z, c = lax.axis_index("grp") // 2, lax.axis_index("col")
    tiles = s_ref.shape[0] // K_TILE
    spans = [pl.ds(k * K_TILE, K_TILE) for k in range(tiles)]
    copies = [pltpu.make_async_copy(s_hbm.at[span], s_ref.at[span], sems.at[k]) for k, span in enumerate(spans)]
    for copy in copies:
        copy.start()
    for k, span in enumerate(spans):
        copies[k].wait()
        lhs = jnp.concatenate([ref[:, span] for ref in pieces], axis=0)
        term = jnp.dot(lhs, s_ref[span, :], preferred_element_type=jnp.float32)
        if k == 0:
            total[...] = term
        elif k < tiles - 1:
            total[...] += term
        else:
            term += total[...]
    rows, cols = outs[0].shape[1:]
    for i, place in enumerate(PLACES):
        slot = slot_of(z, c // 4, c // 2 % 2, c % 2, *place)
        for half in range(2):
            outs[half][slot] = term[i * rows : (i + 1) * rows, half * cols : (half + 1) * cols]


def product(pieces, s_both):
    rows, blk = pieces[0].shape
    cols = s_both.shape[1]
    block_rows = rows * len(pieces) // len(PLACES)
    whole = pl.BlockSpec(memory_space=pltpu.VMEM)
    return pl.pallas_call(
        product_kernel,
        out_shape=[jax.ShapeDtypeStruct((len(PLACES), block_rows, cols // 2), jnp.float32)] * 2,
        in_specs=[whole] * len(pieces) + [pl.BlockSpec(memory_space=pltpu.HBM)],
        out_specs=[whole] * 2,
        scratch_shapes=[
            pltpu.VMEM((len(PLACES) * block_rows, cols), jnp.float32),
            pltpu.VMEM((blk, cols), jnp.bfloat16),
            pltpu.SemaphoreType.DMA((blk // K_TILE,)),
        ],
        compiler_params=pltpu.CompilerParams(vmem_limit_bytes=20 * 2**20),
    )(*pieces, s_both)


def col_move(value, target):
    pairs = []
    for c in range(16):
        x, y, core = c // 4, c // 2 % 2, c % 2
        tx, ty, tcore = target(x, y, core)
        pairs.append((c, tx % 4 * 4 + ty * 2 + tcore))
    return lax.ppermute(value, "col", pairs)


def slice_move(value, target):
    pairs = []
    for g in range(32):
        for c in range(16):
            to = target(g // 2, g % 2, c)
            if to is not None:
                pairs.append((g * 16 + c, (to[0] % 16 * 2 + to[1]) * 16 + to[2]))
    return lax.ppermute(value, ("grp", "col"), pairs)


def exchange(step, z, y_hi, c):
    even = (c - z) % 2 == 0
    return (z + 1 if even == (step % 2 == 1) else z - 1, y_hi, c)


def combine_kernel(count, *refs):
    own_ref, arrived_ref = refs[0], refs[1]
    outs = refs[len(refs) - count :]
    outs[0][...] = own_ref[...] + arrived_ref[...]
    if count == 2:
        outs[1][...] = refs[2][...]


def combine(own, arrived, following, after):
    count = 1 if following is None else 2
    arrays = [own, arrived] + ([] if following is None else [following])
    whole = pl.BlockSpec(memory_space=pltpu.VMEM)
    return pl.pallas_call(
        functools.partial(combine_kernel, count),
        out_shape=[jax.ShapeDtypeStruct(own.shape, own.dtype)] * count,
        in_specs=[whole] * len(arrays) + [pl.BlockSpec(memory_space=pl.ANY)],
        out_specs=[whole] * count,
        compiler_params=pltpu.CompilerParams(vmem_limit_bytes=4 * 2**20),
    )(*arrays, after)


def gather_col(here):
    pieces = {(0, 0): here}
    for d in (1, 3, 2):
        pieces[d, 0] = col_move(here, lambda x, y, k, d=d: (x - d, y, k))
    pieces[0, 1] = col_move(here, lambda x, y, k: (x, 1 - y, k))
    pieces[2, 1] = col_move(pieces[0, 1], lambda x, y, k: (x - 2, y, k))
    for d in (1, 3):
        pieces[d, 1] = col_move(pieces[d, 0], lambda x, y, k: (x, 1 - y, k))
    return pieces


def per_device(window_rows, secular, source, kept_count):
    blk = secular.shape[0]
    g = lax.axis_index("grp")
    c = lax.axis_index("col")
    z, y_hi = g // 2, g % 2
    is_odd = (c + z) % 2 == 1
    own_base = g * blk
    partner_base = jnp.bitwise_xor(g, 16) * blk

    other = col_move(secular, lambda x, y, k: (x, y, 1 - k))
    inside = (source >= own_base) & (source < own_base + blk)
    place = jnp.where(inside, source - own_base, blk + source - partner_base)
    *parts, flag = scatter_rows(place, window_rows.T)
    own_parts, cross_parts = parts[:CHUNKS], parts[CHUNKS:]
    s_both, masked = split_halves(kept_count, flag, secular, other)

    pieces = []
    leaving, after = cross_parts[0], masked
    for h in range(CHUNKS):
        arrived = lax.ppermute(leaving, "grp", [(i, i ^ 16) for i in range(32)])
        here, *next_leaving = combine(own_parts[h], arrived, cross_parts[h + 1] if h + 1 < CHUNKS else None, after)
        if next_leaving:
            leaving = next_leaving[0]
        gathered = gather_col(here)
        pieces.append(gathered)
        after = gathered[2, 1]
    pieces = [gathered[p] for p in PLACES for gathered in pieces]

    s_both = pltpu.with_memory_space_constraint(s_both, pltpu.HBM)
    terms = product(pieces, s_both)
    moving = [term[0] for term in terms]
    for step in range(1, 8):
        for half in range(2):
            moving[half] = terms[half][step] + slice_move(moving[half], functools.partial(exchange, step))

    mine, theirs = moving
    rows = mine.shape[0] // 2

    def part(value, y):
        return jnp.where(y == 1, value[rows:], value[:rows])

    def odd_or_even(when_odd, when_even):
        def target(z, y_hi, c):
            is_odd = (c - z) % 2
            flips = when_odd if is_odd else when_even
            return None if flips is None else (z + is_odd, y_hi ^ flips[0], c ^ flips[1])

        return target

    mine_here, mine_across = part(mine, y_hi), part(mine, 1 - y_hi)
    theirs_here, theirs_across = part(theirs, y_hi), part(theirs, 1 - y_hi)
    total = slice_move(theirs_across, odd_or_even((1, 1), None))
    total += slice_move(jnp.where(is_odd, mine_here, theirs_here), odd_or_even((0, 0), (0, 1)))
    total += slice_move(jnp.where(is_odd, mine_across, theirs_across), odd_or_even((1, 0), (1, 1)))
    total += slice_move(jnp.where(is_odd, theirs_here, mine_across), odd_or_even((0, 1), (1, 0)))
    final = jnp.where(is_odd, total, total + mine_here).astype(jnp.bfloat16)
    return final.reshape(rows, 2, -1).transpose(1, 0, 2)


def solution(mesh):
    return jax.shard_map(
        per_device,
        mesh=mesh,
        in_specs=(P("grp", "col"), P("grp", "col"), P("grp"), P()),
        out_specs=P(None, "grp", "col"),
        check_vma=False,
    )
```

```python
import functools

import jax
import jax.numpy as jnp
from jax import lax
from jax.experimental import pallas as pl
from jax.experimental.pallas import tpu as pltpu
from jax.sharding import PartitionSpec as P

LANES = 128
UNROLL = 32
K_TILE = 768
CHUNKS = 2
PLACES = ((0, 0), (1, 0), (3, 0), (2, 0), (0, 1), (2, 1), (1, 1), (3, 1))


def scatter_kernel(place_ref, w_ref, *refs):
    outs, flag_ref, rows, spread = refs[:-3], refs[-3], refs[-2], refs[-1]
    width, blk = w_ref.shape
    part_rows = width // CHUNKS
    ones = jnp.ones((LANES - width, LANES), jnp.float32)
    spread[...] = jnp.zeros_like(spread)
    for at in range(0, blk, LANES):
        part = w_ref[:, at : at + LANES].astype(jnp.float32)
        rows[at : at + LANES, :] = jnp.concatenate([part, ones], axis=0).T

    def move(i, carry):
        for u in range(UNROLL):
            j = i * UNROLL + u
            spread[pl.ds(place_ref[j], 1), :] = rows[pl.ds(j, 1), :]
        return carry

    lax.fori_loop(0, blk // UNROLL, move, 0)
    for side in range(2):
        for at in range(0, blk, LANES):
            block = spread[side * blk + at : side * blk + at + LANES, :]
            turned = block.T[:width].astype(jnp.bfloat16)
            for h in range(CHUNKS):
                outs[side * CHUNKS + h][:, at : at + LANES] = turned[h * part_rows : (h + 1) * part_rows]
            if side == 0:
                mark = block[:, width:]
                flag_ref[at : at + LANES, :] = jnp.concatenate([mark, mark], axis=1).astype(jnp.bfloat16)


def scatter_rows(place, w_t):
    width, blk = w_t.shape
    return pl.pallas_call(
        scatter_kernel,
        out_shape=[jax.ShapeDtypeStruct((width // CHUNKS, blk), jnp.bfloat16)] * (2 * CHUNKS)
        + [jax.ShapeDtypeStruct((blk, LANES), jnp.bfloat16)],
        in_specs=[pl.BlockSpec(memory_space=pltpu.SMEM), pl.BlockSpec(memory_space=pltpu.VMEM)],
        out_specs=[pl.BlockSpec(memory_space=pltpu.VMEM)] * (2 * CHUNKS + 1),
        scratch_shapes=[pltpu.VMEM((blk, LANES), jnp.float32), pltpu.VMEM((2 * blk, LANES), jnp.float32)],
        compiler_params=pltpu.CompilerParams(vmem_limit_bytes=16 * 2**20),
    )(place, w_t)


def halves_kernel(kept_ref, flag_ref, own_ref, other_ref, out_ref, done_ref):
    tile, cols = own_ref.shape
    g = lax.axis_index("grp")
    base = (g * pl.num_programs(0) + pl.program_id(0)) * tile
    row = lax.broadcasted_iota(jnp.int32, (tile, LANES), 0) + base
    done_ref[...] = jnp.zeros_like(done_ref)
    mark = flag_ref[...].astype(jnp.float32)
    alive = row < kept_ref[0]
    mine = alive & (mark > 0.5)
    theirs = alive & (mark < 0.5)
    lower = g >= 16
    in_half = (
        jnp.where(lower, theirs.astype(jnp.float32), mine.astype(jnp.float32)),
        jnp.where(lower, mine.astype(jnp.float32), theirs.astype(jnp.float32)),
    )
    for c, ref in enumerate((own_ref, other_ref)):
        for h in range(2):
            for v in range(cols // LANES):
                values = ref[:, v * LANES : (v + 1) * LANES].astype(jnp.float32)
                at = (c * 2 + h) * cols + v * LANES
                out_ref[:, at : at + LANES] = jnp.where(in_half[h] > 0.5, values, 0.0).astype(jnp.bfloat16)


def split_halves(kept, flag, own, other):
    blk, cols = own.shape
    return pl.pallas_call(
        halves_kernel,
        grid=(blk // K_TILE,),
        out_shape=[
            jax.ShapeDtypeStruct((blk, 4 * cols), jnp.bfloat16),
            jax.ShapeDtypeStruct((8, LANES), jnp.float32),
        ],
        in_specs=[
            pl.BlockSpec(memory_space=pltpu.SMEM),
            pl.BlockSpec((K_TILE, LANES), lambda i: (i, 0)),
            pl.BlockSpec((K_TILE, cols), lambda i: (i, 0)),
            pl.BlockSpec((K_TILE, cols), lambda i: (i, 0)),
        ],
        out_specs=[pl.BlockSpec((K_TILE, 4 * cols), lambda i: (i, 0)), pl.BlockSpec((8, LANES), lambda i: (0, 0))],
        compiler_params=pltpu.CompilerParams(vmem_limit_bytes=12 * 2**20),
    )(kept, flag, own, other)


def slot_of(z, x, y_lo, core, dx, dy):
    odd = (core + z) % 2
    target = (x + dx) % 4 * 4 + (y_lo + dy) % 2 * 2 + core
    above = (target + 16 - z - odd) % 16 // 2
    even_slot = jnp.where(above > 4, 2 * above - 9, jnp.minimum(8 - 2 * above, 7))
    odd_slot = jnp.where(above > 4, 2 * above - 8, jnp.maximum(7 - 2 * above, 0))
    return jnp.where(odd == 1, odd_slot, even_slot)


def product_kernel(*refs):
    count = len(refs) - 6
    pieces, s_hbm, outs = refs[:count], refs[count], refs[count + 1 : count + 3]
    total, s_ref, sems = refs[count + 3 :]
    z, c = lax.axis_index("grp") // 2, lax.axis_index("col")
    tiles = s_ref.shape[0] // K_TILE
    spans = [pl.ds(k * K_TILE, K_TILE) for k in range(tiles)]
    copies = [pltpu.make_async_copy(s_hbm.at[span], s_ref.at[span], sems.at[k]) for k, span in enumerate(spans)]
    for copy in copies:
        copy.start()
    for k, span in enumerate(spans):
        copies[k].wait()
        lhs = jnp.concatenate([ref[:, span] for ref in pieces], axis=0)
        term = jnp.dot(lhs, s_ref[span, :], preferred_element_type=jnp.float32)
        if k == 0:
            total[...] = term
        elif k < tiles - 1:
            total[...] += term
        else:
            term += total[...]
    rows, cols = outs[0].shape[1:]
    for i, place in enumerate(PLACES):
        slot = slot_of(z, c // 4, c // 2 % 2, c % 2, *place)
        for half in range(2):
            outs[half][slot] = term[i * rows : (i + 1) * rows, half * cols : (half + 1) * cols]


def product(pieces, s_both):
    rows, blk = pieces[0].shape
    cols = s_both.shape[1]
    block_rows = rows * len(pieces) // len(PLACES)
    whole = pl.BlockSpec(memory_space=pltpu.VMEM)
    return pl.pallas_call(
        product_kernel,
        out_shape=[jax.ShapeDtypeStruct((len(PLACES), block_rows, cols // 2), jnp.float32)] * 2,
        in_specs=[whole] * len(pieces) + [pl.BlockSpec(memory_space=pltpu.HBM)],
        out_specs=[whole] * 2,
        scratch_shapes=[
            pltpu.VMEM((len(PLACES) * block_rows, cols), jnp.float32),
            pltpu.VMEM((blk, cols), jnp.bfloat16),
            pltpu.SemaphoreType.DMA((blk // K_TILE,)),
        ],
        compiler_params=pltpu.CompilerParams(vmem_limit_bytes=20 * 2**20),
    )(*pieces, s_both)


def col_move(value, target):
    pairs = []
    for c in range(16):
        x, y, core = c // 4, c // 2 % 2, c % 2
        tx, ty, tcore = target(x, y, core)
        pairs.append((c, tx % 4 * 4 + ty * 2 + tcore))
    return lax.ppermute(value, "col", pairs)


def slice_move(value, target):
    pairs = []
    for g in range(32):
        for c in range(16):
            to = target(g // 2, g % 2, c)
            if to is not None:
                pairs.append((g * 16 + c, (to[0] % 16 * 2 + to[1]) * 16 + to[2]))
    return lax.ppermute(value, ("grp", "col"), pairs)


def exchange(step, z, y_hi, c):
    even = (c - z) % 2 == 0
    return (z + 1 if even == (step % 2 == 1) else z - 1, y_hi, c)


def combine_kernel(count, *refs):
    own_ref, arrived_ref = refs[0], refs[1]
    outs = refs[len(refs) - count :]
    outs[0][...] = own_ref[...] + arrived_ref[...]
    if count == 2:
        outs[1][...] = refs[2][...]


def combine(own, arrived, following, *after):
    count = 1 if following is None else 2
    arrays = [own, arrived] + ([] if following is None else [following])
    whole = pl.BlockSpec(memory_space=pltpu.VMEM)
    return pl.pallas_call(
        functools.partial(combine_kernel, count),
        out_shape=[jax.ShapeDtypeStruct(own.shape, own.dtype)] * count,
        in_specs=[whole] * len(arrays) + [pl.BlockSpec(memory_space=pl.ANY)] * len(after),
        out_specs=[whole] * count,
        compiler_params=pltpu.CompilerParams(vmem_limit_bytes=4 * 2**20),
    )(*arrays, *after)


def gather_col(here, direct):
    pieces = {(0, 0): here}
    for d in (1, 3, 2):
        pieces[d, 0] = col_move(here, lambda x, y, k, d=d: (x - d, y, k))
    pieces[0, 1] = col_move(here, lambda x, y, k: (x, 1 - y, k))
    if direct:
        for d in (1, 3, 2):
            pieces[d, 1] = col_move(here, lambda x, y, k, d=d: (x - d, 1 - y, k))
    else:
        pieces[2, 1] = col_move(pieces[0, 1], lambda x, y, k: (x - 2, y, k))
        for d in (1, 3):
            pieces[d, 1] = col_move(pieces[d, 0], lambda x, y, k: (x, 1 - y, k))
    return pieces


def per_device(window_rows, secular, source, kept_count):
    blk = secular.shape[0]
    g = lax.axis_index("grp")
    c = lax.axis_index("col")
    z, y_hi = g // 2, g % 2
    is_odd = (c + z) % 2 == 1
    own_base = g * blk
    partner_base = jnp.bitwise_xor(g, 16) * blk

    other = col_move(secular, lambda x, y, k: (x, y, 1 - k))
    inside = (source >= own_base) & (source < own_base + blk)
    place = jnp.where(inside, source - own_base, blk + source - partner_base)
    *parts, flag = scatter_rows(place, window_rows.T)
    own_parts, cross_parts = parts[:CHUNKS], parts[CHUNKS:]
    s_both, masked = split_halves(kept_count, flag, secular, other)

    pieces = []
    leaving, after = cross_parts[0], [masked]
    for h in range(CHUNKS):
        arrived = lax.ppermute(leaving, "grp", [(i, i ^ 16) for i in range(32)])
        here, *next_leaving = combine(own_parts[h], arrived, cross_parts[h + 1] if h + 1 < CHUNKS else None, *after)
        if next_leaving:
            leaving = next_leaving[0]
        gathered = gather_col(here, h + 1 < CHUNKS)
        pieces.append(gathered)
        after = [gathered[2, 0], gathered[2, 1]]
    pieces = [gathered[p] for p in PLACES for gathered in pieces]

    s_both = pltpu.with_memory_space_constraint(s_both, pltpu.HBM)
    terms = product(pieces, s_both)
    moving = [term[0] for term in terms]
    for step in range(1, 8):
        for half in range(2):
            moving[half] = terms[half][step] + slice_move(moving[half], functools.partial(exchange, step))

    mine, theirs = moving
    rows = mine.shape[0] // 2

    def part(value, y):
        return jnp.where(y == 1, value[rows:], value[:rows])

    def odd_or_even(when_odd, when_even):
        def target(z, y_hi, c):
            is_odd = (c - z) % 2
            flips = when_odd if is_odd else when_even
            return None if flips is None else (z + is_odd, y_hi ^ flips[0], c ^ flips[1])

        return target

    mine_here, mine_across = part(mine, y_hi), part(mine, 1 - y_hi)
    theirs_here, theirs_across = part(theirs, y_hi), part(theirs, 1 - y_hi)
    total = slice_move(theirs_across, odd_or_even((1, 1), None))
    total += slice_move(jnp.where(is_odd, mine_here, theirs_here), odd_or_even((0, 0), (0, 1)))
    total += slice_move(jnp.where(is_odd, mine_across, theirs_across), odd_or_even((1, 0), (1, 1)))
    total += slice_move(jnp.where(is_odd, theirs_here, mine_across), odd_or_even((0, 1), (1, 0)))
    final = jnp.where(is_odd, total, total + mine_here).astype(jnp.bfloat16)
    return final.reshape(rows, 2, -1).transpose(1, 0, 2)


def solution(mesh):
    return jax.shard_map(
        per_device,
        mesh=mesh,
        in_specs=(P("grp", "col"), P("grp", "col"), P("grp"), P()),
        out_specs=P(None, "grp", "col"),
        check_vma=False,
    )
```

```python
import functools

import jax
import jax.numpy as jnp
from jax import lax
from jax.experimental import pallas as pl
from jax.experimental.pallas import tpu as pltpu
from jax.sharding import PartitionSpec as P

LANES = 128
UNROLL = 32
K_TILE = 768
CHUNKS = 2
PLACES = ((0, 0), (1, 0), (3, 0), (2, 0), (0, 1), (2, 1), (1, 1), (3, 1))


def scatter_kernel(place_ref, w_ref, *refs):
    outs, flag_ref, rows, spread = refs[:-3], refs[-3], refs[-2], refs[-1]
    width, blk = w_ref.shape
    part_rows = width // CHUNKS
    ones = jnp.ones((LANES - width, LANES), jnp.float32)
    spread[...] = jnp.zeros_like(spread)
    for at in range(0, blk, LANES):
        part = w_ref[:, at : at + LANES].astype(jnp.float32)
        rows[at : at + LANES, :] = jnp.concatenate([part, ones], axis=0).T

    def move(i, carry):
        for u in range(UNROLL):
            j = i * UNROLL + u
            spread[pl.ds(place_ref[j], 1), :] = rows[pl.ds(j, 1), :]
        return carry

    lax.fori_loop(0, blk // UNROLL, move, 0)
    for side in range(2):
        for at in range(0, blk, LANES):
            block = spread[side * blk + at : side * blk + at + LANES, :]
            turned = block.T[:width].astype(jnp.bfloat16)
            for h in range(CHUNKS):
                outs[side * CHUNKS + h][:, at : at + LANES] = turned[h * part_rows : (h + 1) * part_rows]
            if side == 0:
                mark = block[:, width:]
                flag_ref[at : at + LANES, :] = jnp.concatenate([mark, mark], axis=1).astype(jnp.bfloat16)


def scatter_rows(place, w_t):
    width, blk = w_t.shape
    return pl.pallas_call(
        scatter_kernel,
        out_shape=[jax.ShapeDtypeStruct((width // CHUNKS, blk), jnp.bfloat16)] * (2 * CHUNKS)
        + [jax.ShapeDtypeStruct((blk, LANES), jnp.bfloat16)],
        in_specs=[pl.BlockSpec(memory_space=pltpu.SMEM), pl.BlockSpec(memory_space=pltpu.VMEM)],
        out_specs=[pl.BlockSpec(memory_space=pltpu.VMEM)] * (2 * CHUNKS + 1),
        scratch_shapes=[pltpu.VMEM((blk, LANES), jnp.float32), pltpu.VMEM((2 * blk, LANES), jnp.float32)],
        compiler_params=pltpu.CompilerParams(vmem_limit_bytes=16 * 2**20),
    )(place, w_t)


def halves_kernel(kept_ref, flag_ref, own_ref, other_ref, out_ref, done_ref):
    tile, cols = own_ref.shape
    g = lax.axis_index("grp")
    base = (g * pl.num_programs(0) + pl.program_id(0)) * tile
    row = lax.broadcasted_iota(jnp.int32, (tile, LANES), 0) + base
    done_ref[...] = jnp.zeros_like(done_ref)
    mark = flag_ref[...].astype(jnp.float32)
    alive = row < kept_ref[0]
    mine = alive & (mark > 0.5)
    theirs = alive & (mark < 0.5)
    lower = g >= 16
    in_half = (
        jnp.where(lower, theirs.astype(jnp.float32), mine.astype(jnp.float32)),
        jnp.where(lower, mine.astype(jnp.float32), theirs.astype(jnp.float32)),
    )
    for c, ref in enumerate((own_ref, other_ref)):
        for h in range(2):
            for v in range(cols // LANES):
                values = ref[:, v * LANES : (v + 1) * LANES].astype(jnp.float32)
                at = (c * 2 + h) * cols + v * LANES
                out_ref[:, at : at + LANES] = jnp.where(in_half[h] > 0.5, values, 0.0).astype(jnp.bfloat16)


def split_halves(kept, flag, own, other):
    blk, cols = own.shape
    return pl.pallas_call(
        halves_kernel,
        grid=(blk // K_TILE,),
        out_shape=[
            jax.ShapeDtypeStruct((blk, 4 * cols), jnp.bfloat16),
            jax.ShapeDtypeStruct((8, LANES), jnp.float32),
        ],
        in_specs=[
            pl.BlockSpec(memory_space=pltpu.SMEM),
            pl.BlockSpec((K_TILE, LANES), lambda i: (i, 0)),
            pl.BlockSpec((K_TILE, cols), lambda i: (i, 0)),
            pl.BlockSpec((K_TILE, cols), lambda i: (i, 0)),
        ],
        out_specs=[pl.BlockSpec((K_TILE, 4 * cols), lambda i: (i, 0)), pl.BlockSpec((8, LANES), lambda i: (0, 0))],
        compiler_params=pltpu.CompilerParams(vmem_limit_bytes=12 * 2**20),
    )(kept, flag, own, other)


def slot_of(z, x, y_lo, core, dx, dy):
    odd = (core + z) % 2
    target = (x + dx) % 4 * 4 + (y_lo + dy) % 2 * 2 + core
    above = (target + 16 - z - odd) % 16 // 2
    even_slot = jnp.where(above > 4, 2 * above - 9, jnp.minimum(8 - 2 * above, 7))
    odd_slot = jnp.where(above > 4, 2 * above - 8, jnp.maximum(7 - 2 * above, 0))
    return jnp.where(odd == 1, odd_slot, even_slot)


def product_kernel(*refs):
    count = len(refs) - 5
    pieces = refs[:count]
    s_hbm, out_ref, total, s_ref, sems = refs[count:]
    z, c = lax.axis_index("grp") // 2, lax.axis_index("col")
    tiles = s_ref.shape[0] // K_TILE
    spans = [pl.ds(k * K_TILE, K_TILE) for k in range(tiles)]
    copies = [pltpu.make_async_copy(s_hbm.at[span], s_ref.at[span], sems.at[k]) for k, span in enumerate(spans)]
    for copy in copies:
        copy.start()
    for k, span in enumerate(spans):
        copies[k].wait()
        lhs = jnp.concatenate([ref[:, span] for ref in pieces], axis=0)
        term = jnp.dot(lhs, s_ref[span, :], preferred_element_type=jnp.float32)
        if k == 0:
            total[...] = term
        elif k < tiles - 1:
            total[...] += term
        else:
            term += total[...]
    rows = out_ref.shape[1]
    for i, place in enumerate(PLACES):
        slot = slot_of(z, c // 4, c // 2 % 2, c % 2, *place)
        out_ref[slot] = term[i * rows : (i + 1) * rows, :]


def product(pieces, s_both):
    rows, blk = pieces[0].shape
    cols = s_both.shape[1]
    block_rows = rows * len(pieces) // len(PLACES)
    whole = pl.BlockSpec(memory_space=pltpu.VMEM)
    return pl.pallas_call(
        product_kernel,
        out_shape=jax.ShapeDtypeStruct((len(PLACES), block_rows, cols), jnp.float32),
        in_specs=[whole] * len(pieces) + [pl.BlockSpec(memory_space=pltpu.HBM)],
        out_specs=whole,
        scratch_shapes=[
            pltpu.VMEM((len(PLACES) * block_rows, cols), jnp.float32),
            pltpu.VMEM((blk, cols), jnp.bfloat16),
            pltpu.SemaphoreType.DMA((blk // K_TILE,)),
        ],
        compiler_params=pltpu.CompilerParams(vmem_limit_bytes=20 * 2**20),
    )(*pieces, s_both)


def col_move(value, target):
    pairs = []
    for c in range(16):
        x, y, core = c // 4, c // 2 % 2, c % 2
        tx, ty, tcore = target(x, y, core)
        pairs.append((c, tx % 4 * 4 + ty * 2 + tcore))
    return lax.ppermute(value, "col", pairs)


def slice_move(value, target):
    pairs = []
    for g in range(32):
        for c in range(16):
            to = target(g // 2, g % 2, c)
            if to is not None:
                pairs.append((g * 16 + c, (to[0] % 16 * 2 + to[1]) * 16 + to[2]))
    return lax.ppermute(value, ("grp", "col"), pairs)


def exchange(step, z, y_hi, c):
    even = (c - z) % 2 == 0
    return (z + 1 if even == (step % 2 == 1) else z - 1, y_hi, c)


def combine_kernel(count, *refs):
    own_ref, arrived_ref = refs[0], refs[1]
    outs = refs[len(refs) - count :]
    outs[0][...] = own_ref[...] + arrived_ref[...]
    if count == 2:
        outs[1][...] = refs[2][...]


def combine(own, arrived, following, after):
    count = 1 if following is None else 2
    arrays = [own, arrived] + ([] if following is None else [following])
    whole = pl.BlockSpec(memory_space=pltpu.VMEM)
    return pl.pallas_call(
        functools.partial(combine_kernel, count),
        out_shape=[jax.ShapeDtypeStruct(own.shape, own.dtype)] * count,
        in_specs=[whole] * len(arrays) + [pl.BlockSpec(memory_space=pl.ANY)],
        out_specs=[whole] * count,
        compiler_params=pltpu.CompilerParams(vmem_limit_bytes=4 * 2**20),
    )(*arrays, after)


def add_term_kernel(slot, terms_ref, arrived_ref, after_ref, out_ref):
    out_ref[...] = terms_ref[slot] + arrived_ref[...]


def add_term(terms, slot, arrived, after):
    whole = pl.BlockSpec(memory_space=pltpu.VMEM)
    return pl.pallas_call(
        functools.partial(add_term_kernel, slot),
        out_shape=jax.ShapeDtypeStruct(arrived.shape, arrived.dtype),
        in_specs=[whole, whole, pl.BlockSpec(memory_space=pl.ANY)],
        out_specs=whole,
        compiler_params=pltpu.CompilerParams(vmem_limit_bytes=4 * 2**20),
    )(terms, arrived, after)


def gather_col(here):
    pieces = {(0, 0): here}
    for d in (1, 3, 2):
        pieces[d, 0] = col_move(here, lambda x, y, k, d=d: (x - d, y, k))
    pieces[0, 1] = col_move(here, lambda x, y, k: (x, 1 - y, k))
    pieces[2, 1] = col_move(pieces[0, 1], lambda x, y, k: (x - 2, y, k))
    for d in (1, 3):
        pieces[d, 1] = col_move(pieces[d, 0], lambda x, y, k: (x, 1 - y, k))
    return pieces


def per_device(window_rows, secular, source, kept_count):
    blk = secular.shape[0]
    g = lax.axis_index("grp")
    c = lax.axis_index("col")
    z, y_hi = g // 2, g % 2
    is_odd = (c + z) % 2 == 1
    own_base = g * blk
    partner_base = jnp.bitwise_xor(g, 16) * blk

    other = col_move(secular, lambda x, y, k: (x, y, 1 - k))
    inside = (source >= own_base) & (source < own_base + blk)
    place = jnp.where(inside, source - own_base, blk + source - partner_base)
    *parts, flag = scatter_rows(place, window_rows.T)
    own_parts, cross_parts = parts[:CHUNKS], parts[CHUNKS:]
    s_both, masked = split_halves(kept_count, flag, secular, other)

    pieces = []
    leaving, after = cross_parts[0], masked
    for h in range(CHUNKS):
        arrived = lax.ppermute(leaving, "grp", [(i, i ^ 16) for i in range(32)])
        here, *next_leaving = combine(own_parts[h], arrived, cross_parts[h + 1] if h + 1 < CHUNKS else None, after)
        if next_leaving:
            leaving = next_leaving[0]
        gathered = gather_col(here)
        pieces.append(gathered)
        after = gathered[2, 1]
    pieces = [gathered[p] for p in PLACES for gathered in pieces]

    s_both = pltpu.with_memory_space_constraint(s_both, pltpu.HBM)
    terms = product(pieces, s_both)
    outer, inner = terms[0], terms[4]
    for step in range(1, 4):
        outer = terms[step] + slice_move(outer, functools.partial(exchange, step))
        inner = slice_move(inner, functools.partial(exchange, step))
        inner = add_term(terms, 4 + step, inner, outer) if step < 3 else terms[7] + inner
    inner += slice_move(outer, lambda z, y_hi, c: (z + 4 if (c - z) % 2 else z - 4, y_hi, c))

    half_cols = inner.shape[1] // 2
    mine, theirs = inner[:, :half_cols], inner[:, half_cols:]
    rows = mine.shape[0] // 2

    def part(value, y):
        return jnp.where(y == 1, value[rows:], value[:rows])

    def odd_or_even(when_odd, when_even):
        def target(z, y_hi, c):
            is_odd = (c - z) % 2
            flips = when_odd if is_odd else when_even
            return None if flips is None else (z + is_odd, y_hi ^ flips[0], c ^ flips[1])

        return target

    mine_here, mine_across = part(mine, y_hi), part(mine, 1 - y_hi)
    theirs_here, theirs_across = part(theirs, y_hi), part(theirs, 1 - y_hi)
    total = slice_move(theirs_across, odd_or_even((1, 1), None))
    total += slice_move(jnp.where(is_odd, mine_here, theirs_here), odd_or_even((0, 0), (0, 1)))
    total += slice_move(jnp.where(is_odd, mine_across, theirs_across), odd_or_even((1, 0), (1, 1)))
    total += slice_move(jnp.where(is_odd, theirs_here, mine_across), odd_or_even((0, 1), (1, 0)))
    final = jnp.where(is_odd, total, total + mine_here).astype(jnp.bfloat16)
    return final.reshape(rows, 2, -1).transpose(1, 0, 2)


def solution(mesh):
    return jax.shard_map(
        per_device,
        mesh=mesh,
        in_specs=(P("grp", "col"), P("grp", "col"), P("grp"), P()),
        out_specs=P(None, "grp", "col"),
        check_vma=False,
    )
```

```python
import functools

import jax
import jax.numpy as jnp
from jax import lax
from jax.experimental import pallas as pl
from jax.experimental.pallas import tpu as pltpu
from jax.sharding import PartitionSpec as P

LANES = 128
UNROLL = 32
K_TILE = 768
CHUNKS = (64,)
PLACES = ((0, 0), (1, 0), (3, 0), (2, 0), (0, 1), (2, 1), (1, 1), (3, 1))


def scatter_kernel(place_ref, w_ref, *refs):
    outs, flag_ref, rows, spread = refs[:-3], refs[-3], refs[-2], refs[-1]
    width, blk = w_ref.shape
    starts = [sum(CHUNKS[:h]) for h in range(len(CHUNKS))]
    ones = jnp.ones((LANES - width, LANES), jnp.float32)
    spread[...] = jnp.zeros_like(spread)
    for at in range(0, blk, LANES):
        part = w_ref[:, at : at + LANES].astype(jnp.float32)
        rows[at : at + LANES, :] = jnp.concatenate([part, ones], axis=0).T

    def move(i, carry):
        for u in range(UNROLL):
            j = i * UNROLL + u
            spread[pl.ds(place_ref[j], 1), :] = rows[pl.ds(j, 1), :]
        return carry

    lax.fori_loop(0, blk // UNROLL, move, 0)
    for side in range(2):
        for at in range(0, blk, LANES):
            block = spread[side * blk + at : side * blk + at + LANES, :]
            turned = block.T[:width].astype(jnp.bfloat16)
            for h, start in enumerate(starts):
                outs[side * len(CHUNKS) + h][:, at : at + LANES] = turned[start : start + CHUNKS[h]]
            if side == 0:
                mark = block[:, width:]
                flag_ref[at : at + LANES, :] = jnp.concatenate([mark, mark], axis=1).astype(jnp.bfloat16)


def scatter_rows(place, w_t):
    width, blk = w_t.shape
    return pl.pallas_call(
        scatter_kernel,
        out_shape=[jax.ShapeDtypeStruct((rows, blk), jnp.bfloat16) for rows in CHUNKS] * 2
        + [jax.ShapeDtypeStruct((blk, LANES), jnp.bfloat16)],
        in_specs=[pl.BlockSpec(memory_space=pltpu.SMEM), pl.BlockSpec(memory_space=pltpu.VMEM)],
        out_specs=[pl.BlockSpec(memory_space=pltpu.VMEM)] * (2 * len(CHUNKS) + 1),
        scratch_shapes=[pltpu.VMEM((blk, LANES), jnp.float32), pltpu.VMEM((2 * blk, LANES), jnp.float32)],
        compiler_params=pltpu.CompilerParams(vmem_limit_bytes=16 * 2**20),
    )(place, w_t)


def halves_kernel(kept_ref, flag_ref, own_ref, other_ref, out_ref, done_ref):
    tile, cols = own_ref.shape
    g = lax.axis_index("grp")
    base = (g * pl.num_programs(0) + pl.program_id(0)) * tile
    row = lax.broadcasted_iota(jnp.int32, (tile, LANES), 0) + base
    done_ref[...] = jnp.zeros_like(done_ref)
    mark = flag_ref[...].astype(jnp.float32)
    alive = row < kept_ref[0]
    mine = alive & (mark > 0.5)
    theirs = alive & (mark < 0.5)
    lower = g >= 16
    in_half = (
        jnp.where(lower, theirs.astype(jnp.float32), mine.astype(jnp.float32)),
        jnp.where(lower, mine.astype(jnp.float32), theirs.astype(jnp.float32)),
    )
    for c, ref in enumerate((own_ref, other_ref)):
        for h in range(2):
            for v in range(cols // LANES):
                values = ref[:, v * LANES : (v + 1) * LANES].astype(jnp.float32)
                at = (c * 2 + h) * cols + v * LANES
                out_ref[:, at : at + LANES] = jnp.where(in_half[h] > 0.5, values, 0.0).astype(jnp.bfloat16)


def split_halves(kept, flag, own, other):
    blk, cols = own.shape
    return pl.pallas_call(
        halves_kernel,
        grid=(blk // K_TILE,),
        out_shape=[
            jax.ShapeDtypeStruct((blk, 4 * cols), jnp.bfloat16),
            jax.ShapeDtypeStruct((8, LANES), jnp.float32),
        ],
        in_specs=[
            pl.BlockSpec(memory_space=pltpu.SMEM),
            pl.BlockSpec((K_TILE, LANES), lambda i: (i, 0)),
            pl.BlockSpec((K_TILE, cols), lambda i: (i, 0)),
            pl.BlockSpec((K_TILE, cols), lambda i: (i, 0)),
        ],
        out_specs=[pl.BlockSpec((K_TILE, 4 * cols), lambda i: (i, 0)), pl.BlockSpec((8, LANES), lambda i: (0, 0))],
        compiler_params=pltpu.CompilerParams(vmem_limit_bytes=12 * 2**20),
    )(kept, flag, own, other)


def slot_of(z, x, y_lo, core, dx, dy):
    odd = (core + z) % 2
    target = (x + dx) % 4 * 4 + (y_lo + dy) % 2 * 2 + core
    above = (target + 16 - z - odd) % 16 // 2
    even_slot = jnp.where(above > 4, 2 * above - 9, jnp.minimum(8 - 2 * above, 7))
    odd_slot = jnp.where(above > 4, 2 * above - 8, jnp.maximum(7 - 2 * above, 0))
    return jnp.where(odd == 1, odd_slot, even_slot)


def product_kernel(*refs):
    count = len(refs) - 5
    pieces = refs[:count]
    s_hbm, out_ref, total, s_ref, sems = refs[count:]
    z, c = lax.axis_index("grp") // 2, lax.axis_index("col")
    tiles = s_ref.shape[0] // K_TILE
    spans = [pl.ds(k * K_TILE, K_TILE) for k in range(tiles)]
    copies = [pltpu.make_async_copy(s_hbm.at[span], s_ref.at[span], sems.at[k]) for k, span in enumerate(spans)]
    for copy in copies:
        copy.start()
    for k, span in enumerate(spans):
        copies[k].wait()
        lhs = jnp.concatenate([ref[:, span] for ref in pieces], axis=0)
        term = jnp.dot(lhs, s_ref[span, :], preferred_element_type=jnp.float32)
        if k == 0:
            total[...] = term
        elif k < tiles - 1:
            total[...] += term
        else:
            term += total[...]
    rows = out_ref.shape[1]
    for i, place in enumerate(PLACES):
        slot = slot_of(z, c // 4, c // 2 % 2, c % 2, *place)
        out_ref[slot] = term[i * rows : (i + 1) * rows, :]


def product(pieces, s_both):
    blk, cols = s_both.shape
    block_rows = sum(CHUNKS)
    whole = pl.BlockSpec(memory_space=pltpu.VMEM)
    return pl.pallas_call(
        product_kernel,
        out_shape=jax.ShapeDtypeStruct((len(PLACES), block_rows, cols), jnp.float32),
        in_specs=[whole] * len(pieces) + [pl.BlockSpec(memory_space=pltpu.HBM)],
        out_specs=whole,
        scratch_shapes=[
            pltpu.VMEM((len(PLACES) * block_rows, cols), jnp.float32),
            pltpu.VMEM((blk, cols), jnp.bfloat16),
            pltpu.SemaphoreType.DMA((blk // K_TILE,)),
        ],
        compiler_params=pltpu.CompilerParams(vmem_limit_bytes=20 * 2**20),
    )(*pieces, s_both)


def col_move(value, target):
    pairs = []
    for c in range(16):
        x, y, core = c // 4, c // 2 % 2, c % 2
        tx, ty, tcore = target(x, y, core)
        pairs.append((c, tx % 4 * 4 + ty * 2 + tcore))
    return lax.ppermute(value, "col", pairs)


def slice_move(value, target):
    pairs = []
    for g in range(32):
        for c in range(16):
            to = target(g // 2, g % 2, c)
            if to is not None:
                pairs.append((g * 16 + c, (to[0] % 16 * 2 + to[1]) * 16 + to[2]))
    return lax.ppermute(value, ("grp", "col"), pairs)


def exchange(step, z, y_hi, c):
    even = (c - z) % 2 == 0
    return (z + 1 if even == (step % 2 == 1) else z - 1, y_hi, c)


def combine_kernel(count, *refs):
    own_ref, arrived_ref = refs[0], refs[1]
    outs = refs[len(refs) - count :]
    outs[0][...] = own_ref[...] + arrived_ref[...]
    if count == 2:
        outs[1][...] = refs[2][...]


def combine(own, arrived, following, after):
    count = 1 if following is None else 2
    arrays = [own, arrived] + ([] if following is None else [following])
    whole = pl.BlockSpec(memory_space=pltpu.VMEM)
    return pl.pallas_call(
        functools.partial(combine_kernel, count),
        out_shape=[jax.ShapeDtypeStruct(a.shape, a.dtype) for a in arrays[: 2 * count : 2]],
        in_specs=[whole] * len(arrays) + [pl.BlockSpec(memory_space=pl.ANY)],
        out_specs=[whole] * count,
        compiler_params=pltpu.CompilerParams(vmem_limit_bytes=4 * 2**20),
    )(*arrays, after)


def add_term_kernel(slot, terms_ref, arrived_ref, after_ref, out_ref):
    out_ref[...] = terms_ref[slot] + arrived_ref[...]


def add_term(terms, slot, arrived, after):
    whole = pl.BlockSpec(memory_space=pltpu.VMEM)
    return pl.pallas_call(
        functools.partial(add_term_kernel, slot),
        out_shape=jax.ShapeDtypeStruct(arrived.shape, arrived.dtype),
        in_specs=[whole, whole, pl.BlockSpec(memory_space=pl.ANY)],
        out_specs=whole,
        compiler_params=pltpu.CompilerParams(vmem_limit_bytes=4 * 2**20),
    )(terms, arrived, after)


def hold_kernel(value_ref, *refs):
    refs[-1][...] = value_ref[...]


def hold(value, after):
    whole = pl.BlockSpec(memory_space=pltpu.VMEM)
    return pl.pallas_call(
        hold_kernel,
        out_shape=jax.ShapeDtypeStruct(value.shape, value.dtype),
        in_specs=[whole] + [pl.BlockSpec(memory_space=pl.ANY)] * len(after),
        out_specs=whole,
        compiler_params=pltpu.CompilerParams(vmem_limit_bytes=4 * 2**20),
    )(value, *after)


def gather_col(here):
    pieces = {(0, 0): here}
    pieces[0, 1] = col_move(here, lambda x, y, k: (x, 1 - y, k))
    for d in (1, 3):
        pieces[d, 0] = col_move(here, lambda x, y, k, d=d: (x - d, y, k))
        pieces[d, 1] = col_move(pieces[d, 0], lambda x, y, k: (x, 1 - y, k))
    held = hold(here, [pieces[1, 0], pieces[3, 0]])
    pieces[2, 0] = col_move(held, lambda x, y, k: (x - 2, y, k))
    pieces[2, 1] = col_move(pieces[0, 1], lambda x, y, k: (x - 2, y, k))
    return pieces


def per_device(window_rows, secular, source, kept_count):
    blk = secular.shape[0]
    g = lax.axis_index("grp")
    c = lax.axis_index("col")
    z, y_hi = g // 2, g % 2
    is_odd = (c + z) % 2 == 1
    own_base = g * blk
    partner_base = jnp.bitwise_xor(g, 16) * blk

    other = col_move(secular, lambda x, y, k: (x, y, 1 - k))
    inside = (source >= own_base) & (source < own_base + blk)
    place = jnp.where(inside, source - own_base, blk + source - partner_base)
    *parts, flag = scatter_rows(place, window_rows.T)
    own_parts, cross_parts = parts[: len(CHUNKS)], parts[len(CHUNKS) :]
    s_both, masked = split_halves(kept_count, flag, secular, other)

    pieces = []
    leaving = cross_parts[0]
    for h in range(len(CHUNKS)):
        arrived = lax.ppermute(leaving, "grp", [(i, i ^ 16) for i in range(32)])
        here, *next_leaving = combine(own_parts[h], arrived, cross_parts[h + 1] if h + 1 < len(CHUNKS) else None, masked)
        if next_leaving:
            leaving = next_leaving[0]
        gathered = gather_col(here)
        pieces.append(gathered)
    pieces = [gathered[p] for p in PLACES for gathered in pieces]

    s_both = pltpu.with_memory_space_constraint(s_both, pltpu.HBM)
    terms = product(pieces, s_both)
    outer, inner = terms[0], terms[4]
    for step in range(1, 4):
        outer = terms[step] + slice_move(outer, functools.partial(exchange, step))
        inner = slice_move(inner, functools.partial(exchange, step))
        inner = add_term(terms, 4 + step, inner, outer) if step < 3 else terms[7] + inner
    inner += slice_move(outer, lambda z, y_hi, c: (z + 4 if (c - z) % 2 else z - 4, y_hi, c))

    half_cols = inner.shape[1] // 2
    mine, theirs = inner[:, :half_cols], inner[:, half_cols:]
    rows = mine.shape[0] // 2

    def part(value, y):
        return jnp.where(y == 1, value[rows:], value[:rows])

    def odd_or_even(when_odd, when_even):
        def target(z, y_hi, c):
            is_odd = (c - z) % 2
            flips = when_odd if is_odd else when_even
            return None if flips is None else (z + is_odd, y_hi ^ flips[0], c ^ flips[1])

        return target

    mine_here, mine_across = part(mine, y_hi), part(mine, 1 - y_hi)
    theirs_here, theirs_across = part(theirs, y_hi), part(theirs, 1 - y_hi)
    total = slice_move(theirs_across, odd_or_even((1, 1), None))
    total += slice_move(jnp.where(is_odd, mine_here, theirs_here), odd_or_even((0, 0), (0, 1)))
    total += slice_move(jnp.where(is_odd, mine_across, theirs_across), odd_or_even((1, 0), (1, 1)))
    total += slice_move(jnp.where(is_odd, theirs_here, mine_across), odd_or_even((0, 1), (1, 0)))
    final = jnp.where(is_odd, total, total + mine_here).astype(jnp.bfloat16)
    return final.reshape(rows, 2, -1).transpose(1, 0, 2)


def solution(mesh):
    return jax.shard_map(
        per_device,
        mesh=mesh,
        in_specs=(P("grp", "col"), P("grp", "col"), P("grp"), P()),
        out_specs=P(None, "grp", "col"),
        check_vma=False,
    )
```

```python
import functools

import jax
import jax.numpy as jnp
from jax import lax
from jax.experimental import pallas as pl
from jax.experimental.pallas import tpu as pltpu
from jax.sharding import PartitionSpec as P

LANES = 128
UNROLL = 32
K_TILE = 768
CHUNKS = (32, 32)
STARTS = tuple(sum(CHUNKS[:h]) for h in range(len(CHUNKS)))
PEERS = 8


def scatter_kernel(place_ref, w_ref, *refs):
    outs, flag_ref, rows, spread = refs[:-3], refs[-3], refs[-2], refs[-1]
    width, blk = w_ref.shape
    ones = jnp.ones((LANES - width, LANES), jnp.float32)
    spread[...] = jnp.zeros_like(spread)
    for at in range(0, blk, LANES):
        part = w_ref[:, at : at + LANES].astype(jnp.float32)
        rows[at : at + LANES, :] = jnp.concatenate([part, ones], axis=0).T

    def move(i, carry):
        for u in range(UNROLL):
            j = i * UNROLL + u
            spread[pl.ds(place_ref[j], 1), :] = rows[pl.ds(j, 1), :]
        return carry

    lax.fori_loop(0, blk // UNROLL, move, 0)
    for side in range(2):
        for at in range(0, blk, LANES):
            block = spread[side * blk + at : side * blk + at + LANES, :]
            turned = block.T[:width].astype(jnp.bfloat16)
            for h, start in enumerate(STARTS):
                outs[side * len(CHUNKS) + h][:, at : at + LANES] = turned[start : start + CHUNKS[h]]
            if side == 0:
                mark = block[:, width:]
                flag_ref[at : at + LANES, :] = jnp.concatenate([mark, mark], axis=1).astype(jnp.bfloat16)


def scatter_rows(place, w_t):
    width, blk = w_t.shape
    return pl.pallas_call(
        scatter_kernel,
        out_shape=[jax.ShapeDtypeStruct((rows, blk), jnp.bfloat16) for rows in CHUNKS] * 2
        + [jax.ShapeDtypeStruct((blk, LANES), jnp.bfloat16)],
        in_specs=[pl.BlockSpec(memory_space=pltpu.SMEM), pl.BlockSpec(memory_space=pltpu.VMEM)],
        out_specs=[pl.BlockSpec(memory_space=pltpu.VMEM)] * (2 * len(CHUNKS) + 1),
        scratch_shapes=[pltpu.VMEM((blk, LANES), jnp.float32), pltpu.VMEM((2 * blk, LANES), jnp.float32)],
        compiler_params=pltpu.CompilerParams(vmem_limit_bytes=16 * 2**20),
    )(place, w_t)


def halves_kernel(kept_ref, flag_ref, own_ref, other_ref, out_ref, done_ref):
    tile, cols = own_ref.shape
    g = lax.axis_index("grp")
    base = (g * pl.num_programs(0) + pl.program_id(0)) * tile
    row = lax.broadcasted_iota(jnp.int32, (tile, LANES), 0) + base
    done_ref[...] = jnp.zeros_like(done_ref)
    mark = flag_ref[...].astype(jnp.float32)
    alive = row < kept_ref[0]
    mine = alive & (mark > 0.5)
    theirs = alive & (mark < 0.5)
    lower = g >= 16
    in_half = (
        jnp.where(lower, theirs.astype(jnp.float32), mine.astype(jnp.float32)),
        jnp.where(lower, mine.astype(jnp.float32), theirs.astype(jnp.float32)),
    )
    for c, ref in enumerate((own_ref, other_ref)):
        for h in range(2):
            for v in range(cols // LANES):
                values = ref[:, v * LANES : (v + 1) * LANES].astype(jnp.float32)
                at = (c * 2 + h) * cols + v * LANES
                out_ref[:, at : at + LANES] = jnp.where(in_half[h] > 0.5, values, 0.0).astype(jnp.bfloat16)


def split_halves(kept, flag, own, other):
    blk, cols = own.shape
    return pl.pallas_call(
        halves_kernel,
        grid=(blk // K_TILE,),
        out_shape=[
            jax.ShapeDtypeStruct((blk, 4 * cols), jnp.bfloat16),
            jax.ShapeDtypeStruct((8, LANES), jnp.float32),
        ],
        in_specs=[
            pl.BlockSpec(memory_space=pltpu.SMEM),
            pl.BlockSpec((K_TILE, LANES), lambda i: (i, 0)),
            pl.BlockSpec((K_TILE, cols), lambda i: (i, 0)),
            pl.BlockSpec((K_TILE, cols), lambda i: (i, 0)),
        ],
        out_specs=[pl.BlockSpec((K_TILE, 4 * cols), lambda i: (i, 0)), pl.BlockSpec((8, LANES), lambda i: (0, 0))],
        compiler_params=pltpu.CompilerParams(vmem_limit_bytes=12 * 2**20),
    )(kept, flag, own, other)


def slot_of(z, core, peer):
    odd = (core + z) % 2
    target = peer * 2 + core
    above = (target + 16 - z - odd) % 16 // 2
    even_slot = jnp.where(above > 4, 2 * above - 9, jnp.minimum(8 - 2 * above, 7))
    odd_slot = jnp.where(above > 4, 2 * above - 8, jnp.maximum(7 - 2 * above, 0))
    return jnp.where(odd == 1, odd_slot, even_slot)


def product_kernel(*refs):
    count = len(refs) - 5
    pieces = refs[:count]
    s_hbm, out_ref, total, s_ref, sems = refs[count:]
    z, c = lax.axis_index("grp") // 2, lax.axis_index("col")
    tiles = s_ref.shape[0] // K_TILE
    spans = [pl.ds(k * K_TILE, K_TILE) for k in range(tiles)]
    copies = [pltpu.make_async_copy(s_hbm.at[span], s_ref.at[span], sems.at[k]) for k, span in enumerate(spans)]
    for copy in copies:
        copy.start()
    for k, span in enumerate(spans):
        copies[k].wait()
        lhs = jnp.concatenate([ref[:, span] for ref in pieces], axis=0)
        term = jnp.dot(lhs, s_ref[span, :], preferred_element_type=jnp.float32)
        if k == 0:
            total[...] = term
        elif k < tiles - 1:
            total[...] += term
        else:
            term += total[...]
    base = 0
    for rows, start in zip(CHUNKS, STARTS):
        for peer in range(PEERS):
            slot = slot_of(z, c % 2, peer)
            out_ref[slot, start : start + rows, :] = term[base : base + rows, :]
            base += rows


def product(pieces, s_both):
    blk, cols = s_both.shape
    block_rows = sum(CHUNKS)
    whole = pl.BlockSpec(memory_space=pltpu.VMEM)
    return pl.pallas_call(
        product_kernel,
        out_shape=jax.ShapeDtypeStruct((PEERS, block_rows, cols), jnp.float32),
        in_specs=[whole] * len(pieces) + [pl.BlockSpec(memory_space=pltpu.HBM)],
        out_specs=whole,
        scratch_shapes=[
            pltpu.VMEM((PEERS * block_rows, cols), jnp.float32),
            pltpu.VMEM((blk, cols), jnp.bfloat16),
            pltpu.SemaphoreType.DMA((blk // K_TILE,)),
        ],
        compiler_params=pltpu.CompilerParams(vmem_limit_bytes=20 * 2**20),
    )(*pieces, s_both)


def col_move(value, target):
    pairs = []
    for c in range(16):
        x, y, core = c // 4, c // 2 % 2, c % 2
        tx, ty, tcore = target(x, y, core)
        pairs.append((c, tx % 4 * 4 + ty * 2 + tcore))
    return lax.ppermute(value, "col", pairs)


def slice_move(value, target):
    pairs = []
    for g in range(32):
        for c in range(16):
            to = target(g // 2, g % 2, c)
            if to is not None:
                pairs.append((g * 16 + c, (to[0] % 16 * 2 + to[1]) * 16 + to[2]))
    return lax.ppermute(value, ("grp", "col"), pairs)


def exchange(step, z, y_hi, c):
    even = (c - z) % 2 == 0
    return (z + 1 if even == (step % 2 == 1) else z - 1, y_hi, c)


def combine_kernel(count, *refs):
    own_ref, arrived_ref = refs[0], refs[1]
    outs = refs[len(refs) - count :]
    here = own_ref[...] + arrived_ref[...]
    rows = here.shape[0]
    for peer in range(PEERS):
        outs[0][peer * rows : (peer + 1) * rows, :] = here
    if count == 2:
        outs[1][...] = refs[2][...]


def combine(own, arrived, following, after):
    count = 1 if following is None else 2
    arrays = [own, arrived] + ([] if following is None else [following])
    whole = pl.BlockSpec(memory_space=pltpu.VMEM)
    return pl.pallas_call(
        functools.partial(combine_kernel, count),
        out_shape=[jax.ShapeDtypeStruct((PEERS * own.shape[0], own.shape[1]), own.dtype)]
        + [jax.ShapeDtypeStruct(a.shape, a.dtype) for a in arrays[2:]],
        in_specs=[whole] * len(arrays) + [pl.BlockSpec(memory_space=pl.ANY)],
        out_specs=[whole] * count,
        compiler_params=pltpu.CompilerParams(vmem_limit_bytes=8 * 2**20),
    )(*arrays, after)


def add_term_kernel(slot, terms_ref, arrived_ref, after_ref, out_ref):
    out_ref[...] = terms_ref[slot] + arrived_ref[...]


def add_term(terms, slot, arrived, after):
    whole = pl.BlockSpec(memory_space=pltpu.VMEM)
    return pl.pallas_call(
        functools.partial(add_term_kernel, slot),
        out_shape=jax.ShapeDtypeStruct(arrived.shape, arrived.dtype),
        in_specs=[whole, whole, pl.BlockSpec(memory_space=pl.ANY)],
        out_specs=whole,
        compiler_params=pltpu.CompilerParams(vmem_limit_bytes=4 * 2**20),
    )(terms, arrived, after)


def gather_col(copies):
    groups = [[peer * 2 + core for peer in range(PEERS)] for core in range(2)]
    return lax.all_to_all(copies, "col", 0, 0, axis_index_groups=groups, tiled=True)


def per_device(window_rows, secular, source, kept_count):
    blk = secular.shape[0]
    g = lax.axis_index("grp")
    c = lax.axis_index("col")
    z, y_hi = g // 2, g % 2
    is_odd = (c + z) % 2 == 1
    own_base = g * blk
    partner_base = jnp.bitwise_xor(g, 16) * blk

    other = col_move(secular, lambda x, y, k: (x, y, 1 - k))
    inside = (source >= own_base) & (source < own_base + blk)
    place = jnp.where(inside, source - own_base, blk + source - partner_base)
    *parts, flag = scatter_rows(place, window_rows.T)
    own_parts, cross_parts = parts[: len(CHUNKS)], parts[len(CHUNKS) :]
    s_both, masked = split_halves(kept_count, flag, secular, other)

    pieces = []
    leaving = cross_parts[0]
    for h in range(len(CHUNKS)):
        arrived = lax.ppermute(leaving, "grp", [(i, i ^ 16) for i in range(32)])
        here, *next_leaving = combine(own_parts[h], arrived, cross_parts[h + 1] if h + 1 < len(CHUNKS) else None, masked)
        if next_leaving:
            leaving = next_leaving[0]
        pieces.append(gather_col(here))

    s_both = pltpu.with_memory_space_constraint(s_both, pltpu.HBM)
    terms = product(pieces, s_both)
    outer, inner = terms[0], terms[4]
    for step in range(1, 4):
        outer = terms[step] + slice_move(outer, functools.partial(exchange, step))
        inner = slice_move(inner, functools.partial(exchange, step))
        inner = add_term(terms, 4 + step, inner, outer) if step < 3 else terms[7] + inner
    inner += slice_move(outer, lambda z, y_hi, c: (z + 4 if (c - z) % 2 else z - 4, y_hi, c))

    half_cols = inner.shape[1] // 2
    mine, theirs = inner[:, :half_cols], inner[:, half_cols:]
    rows = mine.shape[0] // 2

    def part(value, y):
        return jnp.where(y == 1, value[rows:], value[:rows])

    def odd_or_even(when_odd, when_even):
        def target(z, y_hi, c):
            is_odd = (c - z) % 2
            flips = when_odd if is_odd else when_even
            return None if flips is None else (z + is_odd, y_hi ^ flips[0], c ^ flips[1])

        return target

    mine_here, mine_across = part(mine, y_hi), part(mine, 1 - y_hi)
    theirs_here, theirs_across = part(theirs, y_hi), part(theirs, 1 - y_hi)
    total = slice_move(theirs_across, odd_or_even((1, 1), None))
    total += slice_move(jnp.where(is_odd, mine_here, theirs_here), odd_or_even((0, 0), (0, 1)))
    total += slice_move(jnp.where(is_odd, mine_across, theirs_across), odd_or_even((1, 0), (1, 1)))
    total += slice_move(jnp.where(is_odd, theirs_here, mine_across), odd_or_even((0, 1), (1, 0)))
    final = jnp.where(is_odd, total, total + mine_here).astype(jnp.bfloat16)
    return final.reshape(rows, 2, -1).transpose(1, 0, 2)


def solution(mesh):
    return jax.shard_map(
        per_device,
        mesh=mesh,
        in_specs=(P("grp", "col"), P("grp", "col"), P("grp"), P()),
        out_specs=P(None, "grp", "col"),
        check_vma=False,
    )
```

```python
import functools

import jax
import jax.numpy as jnp
from jax import lax
from jax.experimental import pallas as pl
from jax.experimental.pallas import tpu as pltpu
from jax.sharding import PartitionSpec as P

LANES = 128
UNROLL = 32
K_TILE = 768
OUTER = 3
CHUNKS = (32, 32)
STARTS = tuple(sum(CHUNKS[:h]) for h in range(len(CHUNKS)))
PEERS = 8


def scatter_kernel(place_ref, w_ref, *refs):
    outs, flag_ref, rows, spread = refs[:-3], refs[-3], refs[-2], refs[-1]
    width, blk = w_ref.shape
    ones = jnp.ones((LANES - width, LANES), jnp.float32)
    spread[...] = jnp.zeros_like(spread)
    for at in range(0, blk, LANES):
        part = w_ref[:, at : at + LANES].astype(jnp.float32)
        rows[at : at + LANES, :] = jnp.concatenate([part, ones], axis=0).T

    def move(i, carry):
        for u in range(UNROLL):
            j = i * UNROLL + u
            spread[pl.ds(place_ref[j], 1), :] = rows[pl.ds(j, 1), :]
        return carry

    lax.fori_loop(0, blk // UNROLL, move, 0)
    for side in range(2):
        for at in range(0, blk, LANES):
            block = spread[side * blk + at : side * blk + at + LANES, :]
            turned = block.T[:width].astype(jnp.bfloat16)
            for h, start in enumerate(STARTS):
                outs[side * len(CHUNKS) + h][:, at : at + LANES] = turned[start : start + CHUNKS[h]]
            if side == 0:
                mark = block[:, width:]
                flag_ref[at : at + LANES, :] = jnp.concatenate([mark, mark], axis=1).astype(jnp.bfloat16)


def scatter_rows(place, w_t):
    width, blk = w_t.shape
    return pl.pallas_call(
        scatter_kernel,
        out_shape=[jax.ShapeDtypeStruct((rows, blk), jnp.bfloat16) for rows in CHUNKS] * 2
        + [jax.ShapeDtypeStruct((blk, LANES), jnp.bfloat16)],
        in_specs=[pl.BlockSpec(memory_space=pltpu.SMEM), pl.BlockSpec(memory_space=pltpu.VMEM)],
        out_specs=[pl.BlockSpec(memory_space=pltpu.VMEM)] * (2 * len(CHUNKS) + 1),
        scratch_shapes=[pltpu.VMEM((blk, LANES), jnp.float32), pltpu.VMEM((2 * blk, LANES), jnp.float32)],
        compiler_params=pltpu.CompilerParams(vmem_limit_bytes=16 * 2**20),
    )(place, w_t)


def halves_kernel(kept_ref, flag_ref, own_ref, other_ref, out_ref, done_ref):
    tile, cols = own_ref.shape
    g = lax.axis_index("grp")
    base = (g * pl.num_programs(0) + pl.program_id(0)) * tile
    row = lax.broadcasted_iota(jnp.int32, (tile, LANES), 0) + base
    done_ref[...] = jnp.zeros_like(done_ref)
    mark = flag_ref[...].astype(jnp.float32)
    alive = row < kept_ref[0]
    mine = alive & (mark > 0.5)
    theirs = alive & (mark < 0.5)
    lower = g >= 16
    in_half = (
        jnp.where(lower, theirs.astype(jnp.float32), mine.astype(jnp.float32)),
        jnp.where(lower, mine.astype(jnp.float32), theirs.astype(jnp.float32)),
    )
    for c, ref in enumerate((own_ref, other_ref)):
        for h in range(2):
            for v in range(cols // LANES):
                values = ref[:, v * LANES : (v + 1) * LANES].astype(jnp.float32)
                at = (c * 2 + h) * cols + v * LANES
                out_ref[:, at : at + LANES] = jnp.where(in_half[h] > 0.5, values, 0.0).astype(jnp.bfloat16)


def split_halves(kept, flag, own, other):
    blk, cols = own.shape
    return pl.pallas_call(
        halves_kernel,
        grid=(blk // K_TILE,),
        out_shape=[
            jax.ShapeDtypeStruct((blk, 4 * cols), jnp.bfloat16),
            jax.ShapeDtypeStruct((8, LANES), jnp.float32),
        ],
        in_specs=[
            pl.BlockSpec(memory_space=pltpu.SMEM),
            pl.BlockSpec((K_TILE, LANES), lambda i: (i, 0)),
            pl.BlockSpec((K_TILE, cols), lambda i: (i, 0)),
            pl.BlockSpec((K_TILE, cols), lambda i: (i, 0)),
        ],
        out_specs=[pl.BlockSpec((K_TILE, 4 * cols), lambda i: (i, 0)), pl.BlockSpec((8, LANES), lambda i: (0, 0))],
        compiler_params=pltpu.CompilerParams(vmem_limit_bytes=12 * 2**20),
    )(kept, flag, own, other)


def slot_of(z, core, peer):
    odd = (core + z) % 2
    target = peer * 2 + core
    above = (target + 16 - z - odd) % 16 // 2
    even_slot = jnp.where(above > 4, 2 * above - 9, jnp.minimum(8 - 2 * above, 7))
    odd_slot = jnp.where(above > 4, 2 * above - 8, jnp.maximum(7 - 2 * above, 0))
    return jnp.where(odd == 1, odd_slot, even_slot)


def product_kernel(*refs):
    count = len(CHUNKS)
    pieces = refs[:count]
    s_hbm, out_ref, total, lhs_ref, s_ref, sems = refs[count:]
    z, c = lax.axis_index("grp") // 2, lax.axis_index("col")
    tiles = s_ref.shape[0] // K_TILE
    spans = [pl.ds(k * K_TILE, K_TILE) for k in range(tiles)]
    copies = []
    for k, span in enumerate(spans):
        tile = [pltpu.make_async_copy(s_hbm.at[span], s_ref.at[span], sems.at[k, count])]
        for h, (rows, start) in enumerate(zip(CHUNKS, STARTS)):
            there = lhs_ref.at[pl.ds(start * PEERS, rows * PEERS), span]
            tile.append(pltpu.make_async_copy(pieces[h].at[:, span], there, sems.at[k, h]))
        copies.append(tile)
    for tile in copies:
        for copy in tile:
            copy.start()
    for k, span in enumerate(spans):
        for copy in copies[k]:
            copy.wait()
        lhs = lhs_ref[:, span]
        term = jnp.dot(lhs, s_ref[span, :], preferred_element_type=jnp.float32)
        if k == 0:
            total[...] = term
        elif k < tiles - 1:
            total[...] += term
        else:
            term += total[...]
    base = 0
    for rows, start in zip(CHUNKS, STARTS):
        for peer in range(PEERS):
            slot = slot_of(z, c % 2, peer)
            out_ref[slot, start : start + rows, :] = term[base : base + rows, :]
            base += rows


def product(pieces, s_both):
    blk, cols = s_both.shape
    block_rows = sum(CHUNKS)
    hbm = pl.BlockSpec(memory_space=pltpu.HBM)
    return pl.pallas_call(
        product_kernel,
        out_shape=jax.ShapeDtypeStruct((PEERS, block_rows, cols), jnp.float32),
        in_specs=[hbm] * (len(pieces) + 1),
        out_specs=pl.BlockSpec(memory_space=pltpu.VMEM),
        scratch_shapes=[
            pltpu.VMEM((PEERS * block_rows, cols), jnp.float32),
            pltpu.VMEM((PEERS * block_rows, blk), jnp.bfloat16),
            pltpu.VMEM((blk, cols), jnp.bfloat16),
            pltpu.SemaphoreType.DMA((blk // K_TILE, len(CHUNKS) + 1)),
        ],
        compiler_params=pltpu.CompilerParams(vmem_limit_bytes=24 * 2**20),
    )(*pieces, s_both)


def col_move(value, target):
    pairs = []
    for c in range(16):
        x, y, core = c // 4, c // 2 % 2, c % 2
        tx, ty, tcore = target(x, y, core)
        pairs.append((c, tx % 4 * 4 + ty * 2 + tcore))
    return lax.ppermute(value, "col", pairs)


def slice_move(value, target):
    pairs = []
    for g in range(32):
        for c in range(16):
            to = target(g // 2, g % 2, c)
            if to is not None:
                pairs.append((g * 16 + c, (to[0] % 16 * 2 + to[1]) * 16 + to[2]))
    return lax.ppermute(value, ("grp", "col"), pairs)


def exchange(step, z, y_hi, c):
    even = (c - z) % 2 == 0
    return (z + 1 if even == (step % 2 == 1) else z - 1, y_hi, c)


def combine_kernel(*refs):
    own_ref, arrived_ref = refs[0], refs[1]
    here, sems = refs[-2:]
    handed_on = len(refs) == 8
    copies_hbm = refs[4 if handed_on else 3]
    here[...] = own_ref[...] + arrived_ref[...]
    rows = here.shape[0]
    copies = [
        pltpu.make_async_copy(here, copies_hbm.at[pl.ds(peer * rows, rows)], sems.at[peer]) for peer in range(PEERS)
    ]
    for copy in copies:
        copy.start()
    if handed_on:
        refs[5][...] = refs[2][...]
    for copy in copies:
        copy.wait()


def combine(own, arrived, following, after):
    arrays = [own, arrived] + ([] if following is None else [following])
    whole = pl.BlockSpec(memory_space=pltpu.VMEM)
    return pl.pallas_call(
        combine_kernel,
        out_shape=[jax.ShapeDtypeStruct((PEERS * own.shape[0], own.shape[1]), own.dtype)]
        + [jax.ShapeDtypeStruct(a.shape, a.dtype) for a in arrays[2:]],
        in_specs=[whole] * len(arrays) + [pl.BlockSpec(memory_space=pl.ANY)],
        out_specs=[pl.BlockSpec(memory_space=pltpu.HBM)] + [whole] * (len(arrays) - 2),
        scratch_shapes=[pltpu.VMEM(own.shape, own.dtype), pltpu.SemaphoreType.DMA((PEERS,))],
        compiler_params=pltpu.CompilerParams(vmem_limit_bytes=4 * 2**20),
    )(*arrays, after)


def add_term_kernel(slot, terms_ref, arrived_ref, after_ref, out_ref):
    out_ref[...] = terms_ref[slot] + arrived_ref[...]


def add_term(terms, slot, arrived, after):
    whole = pl.BlockSpec(memory_space=pltpu.VMEM)
    return pl.pallas_call(
        functools.partial(add_term_kernel, slot),
        out_shape=jax.ShapeDtypeStruct(arrived.shape, arrived.dtype),
        in_specs=[whole, whole, pl.BlockSpec(memory_space=pl.ANY)],
        out_specs=whole,
        compiler_params=pltpu.CompilerParams(vmem_limit_bytes=4 * 2**20),
    )(terms, arrived, after)


def gather_col(copies):
    groups = [[peer * 2 + core for peer in range(PEERS)] for core in range(2)]
    return lax.all_to_all(copies, "col", 0, 0, axis_index_groups=groups, tiled=True)


def per_device(window_rows, secular, source, kept_count):
    blk = secular.shape[0]
    g = lax.axis_index("grp")
    c = lax.axis_index("col")
    z, y_hi = g // 2, g % 2
    is_odd = (c + z) % 2 == 1
    own_base = g * blk
    partner_base = jnp.bitwise_xor(g, 16) * blk

    other = col_move(secular, lambda x, y, k: (x, y, 1 - k))
    inside = (source >= own_base) & (source < own_base + blk)
    place = jnp.where(inside, source - own_base, blk + source - partner_base)
    *parts, flag = scatter_rows(place, window_rows.T)
    own_parts, cross_parts = parts[: len(CHUNKS)], parts[len(CHUNKS) :]
    s_both, masked = split_halves(kept_count, flag, secular, other)

    pieces = []
    leaving = cross_parts[0]
    for h in range(len(CHUNKS)):
        arrived = lax.ppermute(leaving, "grp", [(i, i ^ 16) for i in range(32)])
        here, *next_leaving = combine(own_parts[h], arrived, cross_parts[h + 1] if h + 1 < len(CHUNKS) else None, masked)
        if next_leaving:
            leaving = next_leaving[0]
        pieces.append(gather_col(here))

    s_both = pltpu.with_memory_space_constraint(s_both, pltpu.HBM)
    pieces = [pltpu.with_memory_space_constraint(piece, pltpu.HBM) for piece in pieces]
    terms = product(pieces, s_both)
    outer, inner = terms[0], terms[OUTER]
    for step in range(1, OUTER):
        outer = terms[step] + slice_move(outer, functools.partial(exchange, step))
        inner = slice_move(inner, functools.partial(exchange, step + OUTER))
        inner = add_term(terms, OUTER + step, inner, outer)
    skipped = slice_move(outer, lambda z, y_hi, c: (z - 5 if (c - z) % 2 else z + 5, y_hi, c))
    for step in range(OUTER, 8 - OUTER):
        inner = terms[OUTER + step] + slice_move(inner, functools.partial(exchange, step + OUTER))
    inner += skipped

    half_cols = inner.shape[1] // 2
    mine, theirs = inner[:, :half_cols], inner[:, half_cols:]
    rows = mine.shape[0] // 2

    def part(value, y):
        return jnp.where(y == 1, value[rows:], value[:rows])

    def odd_or_even(when_odd, when_even):
        def target(z, y_hi, c):
            is_odd = (c - z) % 2
            flips = when_odd if is_odd else when_even
            return None if flips is None else (z + is_odd, y_hi ^ flips[0], c ^ flips[1])

        return target

    mine_here, mine_across = part(mine, y_hi), part(mine, 1 - y_hi)
    theirs_here, theirs_across = part(theirs, y_hi), part(theirs, 1 - y_hi)
    total = slice_move(theirs_across, odd_or_even((1, 1), None))
    total += slice_move(jnp.where(is_odd, mine_here, theirs_here), odd_or_even((0, 0), (0, 1)))
    total += slice_move(jnp.where(is_odd, mine_across, theirs_across), odd_or_even((1, 0), (1, 1)))
    total += slice_move(jnp.where(is_odd, theirs_here, mine_across), odd_or_even((0, 1), (1, 0)))
    final = jnp.where(is_odd, total, total + mine_here).astype(jnp.bfloat16)
    return final.reshape(rows, 2, -1).transpose(1, 0, 2)


def solution(mesh):
    return jax.shard_map(
        per_device,
        mesh=mesh,
        in_specs=(P("grp", "col"), P("grp", "col"), P("grp"), P()),
        out_specs=P(None, "grp", "col"),
        check_vma=False,
    )
```

```python
import functools

import jax
import jax.numpy as jnp
from jax import lax
from jax.experimental import pallas as pl
from jax.experimental.pallas import tpu as pltpu
from jax.sharding import PartitionSpec as P

LANES = 128
UNROLL = 32
K_TILE = 768
CHUNKS = (32, 32)
STARTS = tuple(sum(CHUNKS[:h]) for h in range(len(CHUNKS)))
PEERS = 8


def scatter_kernel(place_ref, w_ref, *refs):
    outs, flag_ref, rows, spread = refs[:-3], refs[-3], refs[-2], refs[-1]
    width, blk = w_ref.shape
    ones = jnp.ones((LANES - width, LANES), jnp.float32)
    spread[...] = jnp.zeros_like(spread)
    for at in range(0, blk, LANES):
        part = w_ref[:, at : at + LANES].astype(jnp.float32)
        rows[at : at + LANES, :] = jnp.concatenate([part, ones], axis=0).T

    def move(i, carry):
        for u in range(UNROLL):
            j = i * UNROLL + u
            spread[pl.ds(place_ref[j], 1), :] = rows[pl.ds(j, 1), :]
        return carry

    lax.fori_loop(0, blk // UNROLL, move, 0)
    for side in range(2):
        for at in range(0, blk, LANES):
            block = spread[side * blk + at : side * blk + at + LANES, :]
            turned = block.T[:width].astype(jnp.bfloat16)
            for h, start in enumerate(STARTS):
                outs[side * len(CHUNKS) + h][:, at : at + LANES] = turned[start : start + CHUNKS[h]]
            if side == 0:
                mark = block[:, width:]
                flag_ref[at : at + LANES, :] = jnp.concatenate([mark, mark], axis=1).astype(jnp.bfloat16)


def scatter_rows(place, w_t):
    width, blk = w_t.shape
    return pl.pallas_call(
        scatter_kernel,
        out_shape=[jax.ShapeDtypeStruct((rows, blk), jnp.bfloat16) for rows in CHUNKS] * 2
        + [jax.ShapeDtypeStruct((blk, LANES), jnp.bfloat16)],
        in_specs=[pl.BlockSpec(memory_space=pltpu.SMEM), pl.BlockSpec(memory_space=pltpu.VMEM)],
        out_specs=[pl.BlockSpec(memory_space=pltpu.VMEM)] * (2 * len(CHUNKS) + 1),
        scratch_shapes=[pltpu.VMEM((blk, LANES), jnp.float32), pltpu.VMEM((2 * blk, LANES), jnp.float32)],
        compiler_params=pltpu.CompilerParams(vmem_limit_bytes=16 * 2**20),
    )(place, w_t)


def halves_kernel(kept_ref, flag_ref, own_ref, other_ref, out_ref, done_ref):
    tile, cols = own_ref.shape
    g = lax.axis_index("grp")
    base = (g * pl.num_programs(0) + pl.program_id(0)) * tile
    row = lax.broadcasted_iota(jnp.int32, (tile, LANES), 0) + base
    done_ref[...] = jnp.zeros_like(done_ref)
    mark = flag_ref[...].astype(jnp.float32)
    alive = row < kept_ref[0]
    mine = alive & (mark > 0.5)
    theirs = alive & (mark < 0.5)
    lower = g >= 16
    in_half = (
        jnp.where(lower, theirs.astype(jnp.float32), mine.astype(jnp.float32)),
        jnp.where(lower, mine.astype(jnp.float32), theirs.astype(jnp.float32)),
    )
    for c, ref in enumerate((own_ref, other_ref)):
        for h in range(2):
            for v in range(cols // LANES):
                values = ref[:, v * LANES : (v + 1) * LANES].astype(jnp.float32)
                at = (c * 2 + h) * cols + v * LANES
                out_ref[:, at : at + LANES] = jnp.where(in_half[h] > 0.5, values, 0.0).astype(jnp.bfloat16)


def split_halves(kept, flag, own, other):
    blk, cols = own.shape
    return pl.pallas_call(
        halves_kernel,
        grid=(blk // K_TILE,),
        out_shape=[
            jax.ShapeDtypeStruct((blk, 4 * cols), jnp.bfloat16),
            jax.ShapeDtypeStruct((8, LANES), jnp.float32),
        ],
        in_specs=[
            pl.BlockSpec(memory_space=pltpu.SMEM),
            pl.BlockSpec((K_TILE, LANES), lambda i: (i, 0)),
            pl.BlockSpec((K_TILE, cols), lambda i: (i, 0)),
            pl.BlockSpec((K_TILE, cols), lambda i: (i, 0)),
        ],
        out_specs=[pl.BlockSpec((K_TILE, 4 * cols), lambda i: (i, 0)), pl.BlockSpec((8, LANES), lambda i: (0, 0))],
        compiler_params=pltpu.CompilerParams(vmem_limit_bytes=12 * 2**20),
    )(kept, flag, own, other)


def slot_of(z, core, peer):
    odd = (core + z) % 2
    target = peer * 2 + core
    above = (target + 16 - z - odd) % 16 // 2
    even_slot = jnp.where(above > 4, 2 * above - 9, jnp.minimum(8 - 2 * above, 7))
    odd_slot = jnp.where(above > 4, 2 * above - 8, jnp.maximum(7 - 2 * above, 0))
    return jnp.where(odd == 1, odd_slot, even_slot)


def product_kernel(piece_hbm, s_hbm, out_ref, total, lhs_ref, s_ref, sems):
    z, c = lax.axis_index("grp") // 2, lax.axis_index("col")
    tiles = s_ref.shape[0] // K_TILE
    spans = [pl.ds(k * K_TILE, K_TILE) for k in range(tiles)]
    copies = [
        (
            pltpu.make_async_copy(s_hbm.at[span], s_ref.at[span], sems.at[k, 0]),
            pltpu.make_async_copy(piece_hbm.at[:, span], lhs_ref.at[:, span], sems.at[k, 1]),
        )
        for k, span in enumerate(spans)
    ]
    for tile in copies:
        for copy in tile:
            copy.start()
    for k, span in enumerate(spans):
        for copy in copies[k]:
            copy.wait()
        term = jnp.dot(lhs_ref[:, span], s_ref[span, :], preferred_element_type=jnp.float32)
        if k == 0:
            total[...] = term
        elif k < tiles - 1:
            total[...] += term
        else:
            term += total[...]
    rows = out_ref.shape[1]
    for peer in range(PEERS):
        out_ref[slot_of(z, c % 2, peer)] = term[peer * rows : (peer + 1) * rows, :]


def product(piece, s_both):
    blk, cols = s_both.shape
    rows = piece.shape[0]
    return pl.pallas_call(
        product_kernel,
        out_shape=jax.ShapeDtypeStruct((PEERS, rows // PEERS, cols), jnp.float32),
        in_specs=[pl.BlockSpec(memory_space=pl.ANY)] * 2,
        out_specs=pl.BlockSpec(memory_space=pltpu.VMEM),
        scratch_shapes=[
            pltpu.VMEM((rows, cols), jnp.float32),
            pltpu.VMEM((rows, blk), jnp.bfloat16),
            pltpu.VMEM((blk, cols), jnp.bfloat16),
            pltpu.SemaphoreType.DMA((blk // K_TILE, 2)),
        ],
        compiler_params=pltpu.CompilerParams(vmem_limit_bytes=20 * 2**20),
    )(piece, s_both)


def col_move(value, target):
    pairs = []
    for c in range(16):
        x, y, core = c // 4, c // 2 % 2, c % 2
        tx, ty, tcore = target(x, y, core)
        pairs.append((c, tx % 4 * 4 + ty * 2 + tcore))
    return lax.ppermute(value, "col", pairs)


def slice_move(value, target):
    pairs = []
    for g in range(32):
        for c in range(16):
            to = target(g // 2, g % 2, c)
            if to is not None:
                pairs.append((g * 16 + c, (to[0] % 16 * 2 + to[1]) * 16 + to[2]))
    return lax.ppermute(value, ("grp", "col"), pairs)


def exchange(step, z, y_hi, c):
    even = (c - z) % 2 == 0
    return (z + 1 if even == (step % 2 == 1) else z - 1, y_hi, c)


def combine_kernel(*refs):
    own_ref, arrived_ref = refs[0], refs[1]
    here, sems = refs[-2:]
    handed_on = len(refs) == 8
    copies_hbm = refs[4 if handed_on else 3]
    here[...] = own_ref[...] + arrived_ref[...]
    rows = here.shape[0]
    copies = [
        pltpu.make_async_copy(here, copies_hbm.at[pl.ds(peer * rows, rows)], sems.at[peer]) for peer in range(PEERS)
    ]
    for copy in copies:
        copy.start()
    if handed_on:
        refs[5][...] = refs[2][...]
    for copy in copies:
        copy.wait()


def combine(own, arrived, following, after):
    arrays = [own, arrived] + ([] if following is None else [following])
    whole = pl.BlockSpec(memory_space=pltpu.VMEM)
    return pl.pallas_call(
        combine_kernel,
        out_shape=[jax.ShapeDtypeStruct((PEERS * own.shape[0], own.shape[1]), own.dtype)]
        + [jax.ShapeDtypeStruct(a.shape, a.dtype) for a in arrays[2:]],
        in_specs=[whole] * len(arrays) + [pl.BlockSpec(memory_space=pl.ANY)],
        out_specs=[pl.BlockSpec(memory_space=pltpu.HBM)] + [whole] * (len(arrays) - 2),
        scratch_shapes=[pltpu.VMEM(own.shape, own.dtype), pltpu.SemaphoreType.DMA((PEERS,))],
        compiler_params=pltpu.CompilerParams(vmem_limit_bytes=4 * 2**20),
    )(*arrays, after)


def add_term_kernel(slot, *refs):
    terms, out_ref = refs[: len(CHUNKS)], refs[-1]
    arrived_ref = refs[len(CHUNKS)] if len(refs) > len(CHUNKS) + 1 else None
    for ref, rows, start in zip(terms, CHUNKS, STARTS):
        value = ref[slot]
        if arrived_ref is not None:
            value += arrived_ref[start : start + rows, :]
        out_ref[start : start + rows, :] = value


def add_term(terms, slot, *arrived):
    whole = pl.BlockSpec(memory_space=pltpu.VMEM)
    return pl.pallas_call(
        functools.partial(add_term_kernel, slot),
        out_shape=jax.ShapeDtypeStruct((sum(CHUNKS), terms[0].shape[2]), jnp.float32),
        in_specs=[whole] * (len(terms) + len(arrived[:1])) + [pl.BlockSpec(memory_space=pl.ANY)] * len(arrived[1:]),
        out_specs=whole,
        compiler_params=pltpu.CompilerParams(vmem_limit_bytes=8 * 2**20),
    )(*terms, *arrived)


def gather_col(copies):
    groups = [[peer * 2 + core for peer in range(PEERS)] for core in range(2)]
    return lax.all_to_all(copies, "col", 0, 0, axis_index_groups=groups, tiled=True)


def per_device(window_rows, secular, source, kept_count):
    blk = secular.shape[0]
    g = lax.axis_index("grp")
    c = lax.axis_index("col")
    z, y_hi = g // 2, g % 2
    is_odd = (c + z) % 2 == 1
    own_base = g * blk
    partner_base = jnp.bitwise_xor(g, 16) * blk

    other = col_move(secular, lambda x, y, k: (x, y, 1 - k))
    inside = (source >= own_base) & (source < own_base + blk)
    place = jnp.where(inside, source - own_base, blk + source - partner_base)
    *parts, flag = scatter_rows(place, window_rows.T)
    own_parts, cross_parts = parts[: len(CHUNKS)], parts[len(CHUNKS) :]
    s_both, masked = split_halves(kept_count, flag, secular, other)

    pieces = []
    leaving = cross_parts[0]
    for h in range(len(CHUNKS)):
        arrived = lax.ppermute(leaving, "grp", [(i, i ^ 16) for i in range(32)])
        here, *next_leaving = combine(own_parts[h], arrived, cross_parts[h + 1] if h + 1 < len(CHUNKS) else None, masked)
        if next_leaving:
            leaving = next_leaving[0]
        pieces.append(gather_col(here))

    s_both = pltpu.with_memory_space_constraint(s_both, pltpu.HBM)
    terms = [product(piece, s_both) for piece in pieces]

    outer, inner = add_term(terms, 0), add_term(terms, 4)
    for step in range(1, 4):
        outer = add_term(terms, step, slice_move(outer, functools.partial(exchange, step)))
        inner = slice_move(inner, functools.partial(exchange, step))
        inner = add_term(terms, 4 + step, inner, *([outer] if step < 3 else []))
    inner += slice_move(outer, lambda z, y_hi, c: (z + 4 if (c - z) % 2 else z - 4, y_hi, c))

    half_cols = inner.shape[1] // 2
    mine, theirs = inner[:, :half_cols], inner[:, half_cols:]
    rows = mine.shape[0] // 2

    def part(value, y):
        return jnp.where(y == 1, value[rows:], value[:rows])

    def odd_or_even(when_odd, when_even):
        def target(z, y_hi, c):
            is_odd = (c - z) % 2
            flips = when_odd if is_odd else when_even
            return None if flips is None else (z + is_odd, y_hi ^ flips[0], c ^ flips[1])

        return target

    mine_here, mine_across = part(mine, y_hi), part(mine, 1 - y_hi)
    theirs_here, theirs_across = part(theirs, y_hi), part(theirs, 1 - y_hi)
    total = slice_move(theirs_across, odd_or_even((1, 1), None))
    total += slice_move(jnp.where(is_odd, mine_here, theirs_here), odd_or_even((0, 0), (0, 1)))
    total += slice_move(jnp.where(is_odd, mine_across, theirs_across), odd_or_even((1, 0), (1, 1)))
    total += slice_move(jnp.where(is_odd, theirs_here, mine_across), odd_or_even((0, 1), (1, 0)))
    final = jnp.where(is_odd, total, total + mine_here).astype(jnp.bfloat16)
    return final.reshape(rows, 2, -1).transpose(1, 0, 2)


def solution(mesh):
    return jax.shard_map(
        per_device,
        mesh=mesh,
        in_specs=(P("grp", "col"), P("grp", "col"), P("grp"), P()),
        out_specs=P(None, "grp", "col"),
        check_vma=False,
    )
```

```python
import functools

import jax
import jax.numpy as jnp
from jax import lax
from jax.experimental import pallas as pl
from jax.experimental.pallas import tpu as pltpu
from jax.sharding import PartitionSpec as P

LANES = 128
UNROLL = 32
K_TILE = 768
CHUNKS = (32, 32)
STARTS = tuple(sum(CHUNKS[:h]) for h in range(len(CHUNKS)))
PEERS = 8


def scatter_kernel(place_ref, w_ref, *refs):
    outs, flag_ref, rows, spread = refs[:-3], refs[-3], refs[-2], refs[-1]
    width, blk = w_ref.shape
    ones = jnp.ones((LANES - width, LANES), jnp.float32)
    spread[...] = jnp.zeros_like(spread)
    for at in range(0, blk, LANES):
        part = w_ref[:, at : at + LANES].astype(jnp.float32)
        rows[at : at + LANES, :] = jnp.concatenate([part, ones], axis=0).T

    def move(i, carry):
        for u in range(UNROLL):
            j = i * UNROLL + u
            spread[pl.ds(place_ref[j], 1), :] = rows[pl.ds(j, 1), :]
        return carry

    lax.fori_loop(0, blk // UNROLL, move, 0)
    for side in range(2):
        for at in range(0, blk, LANES):
            block = spread[side * blk + at : side * blk + at + LANES, :]
            turned = block.T[:width].astype(jnp.bfloat16)
            for h, start in enumerate(STARTS):
                outs[side * len(CHUNKS) + h][:, at : at + LANES] = turned[start : start + CHUNKS[h]]
            if side == 0:
                mark = block[:, width:]
                flag_ref[at : at + LANES, :] = jnp.concatenate([mark, mark], axis=1).astype(jnp.bfloat16)


def scatter_rows(place, w_t):
    width, blk = w_t.shape
    return pl.pallas_call(
        scatter_kernel,
        out_shape=[jax.ShapeDtypeStruct((rows, blk), jnp.bfloat16) for rows in CHUNKS] * 2
        + [jax.ShapeDtypeStruct((blk, LANES), jnp.bfloat16)],
        in_specs=[pl.BlockSpec(memory_space=pltpu.SMEM), pl.BlockSpec(memory_space=pltpu.VMEM)],
        out_specs=[pl.BlockSpec(memory_space=pltpu.VMEM)] * (2 * len(CHUNKS) + 1),
        scratch_shapes=[pltpu.VMEM((blk, LANES), jnp.float32), pltpu.VMEM((2 * blk, LANES), jnp.float32)],
        compiler_params=pltpu.CompilerParams(vmem_limit_bytes=16 * 2**20),
    )(place, w_t)


def halves_kernel(kept_ref, flag_ref, own_ref, other_ref, out_ref, done_ref):
    tile, cols = own_ref.shape
    g = lax.axis_index("grp")
    base = (g * pl.num_programs(0) + pl.program_id(0)) * tile
    row = lax.broadcasted_iota(jnp.int32, (tile, LANES), 0) + base
    done_ref[...] = jnp.zeros_like(done_ref)
    mark = flag_ref[...].astype(jnp.float32)
    alive = row < kept_ref[0]
    mine = alive & (mark > 0.5)
    theirs = alive & (mark < 0.5)
    lower = g >= 16
    in_half = (
        jnp.where(lower, theirs.astype(jnp.float32), mine.astype(jnp.float32)),
        jnp.where(lower, mine.astype(jnp.float32), theirs.astype(jnp.float32)),
    )
    for c, ref in enumerate((own_ref, other_ref)):
        for h in range(2):
            for v in range(cols // LANES):
                values = ref[:, v * LANES : (v + 1) * LANES].astype(jnp.float32)
                at = (c * 2 + h) * cols + v * LANES
                out_ref[:, at : at + LANES] = jnp.where(in_half[h] > 0.5, values, 0.0).astype(jnp.bfloat16)


def split_halves(kept, flag, own, other):
    blk, cols = own.shape
    return pl.pallas_call(
        halves_kernel,
        grid=(blk // K_TILE,),
        out_shape=[
            jax.ShapeDtypeStruct((blk, 4 * cols), jnp.bfloat16),
            jax.ShapeDtypeStruct((8, LANES), jnp.float32),
        ],
        in_specs=[
            pl.BlockSpec(memory_space=pltpu.SMEM),
            pl.BlockSpec((K_TILE, LANES), lambda i: (i, 0)),
            pl.BlockSpec((K_TILE, cols), lambda i: (i, 0)),
            pl.BlockSpec((K_TILE, cols), lambda i: (i, 0)),
        ],
        out_specs=[pl.BlockSpec((K_TILE, 4 * cols), lambda i: (i, 0)), pl.BlockSpec((8, LANES), lambda i: (0, 0))],
        compiler_params=pltpu.CompilerParams(vmem_limit_bytes=12 * 2**20),
    )(kept, flag, own, other)


def slot_of(z, core, peer):
    odd = (core + z) % 2
    target = peer * 2 + core
    above = (target + 16 - z - odd) % 16 // 2
    even_slot = jnp.where(above > 4, 2 * above - 9, jnp.minimum(8 - 2 * above, 7))
    odd_slot = jnp.where(above > 4, 2 * above - 8, jnp.maximum(7 - 2 * above, 0))
    return jnp.where(odd == 1, odd_slot, even_slot)


def product_kernel(*refs):
    count = len(CHUNKS)
    pieces = refs[:count]
    s_hbm, out_ref, total, lhs_ref, s_ref, sems = refs[count:]
    z, c = lax.axis_index("grp") // 2, lax.axis_index("col")
    tiles = s_ref.shape[0] // K_TILE
    spans = [pl.ds(k * K_TILE, K_TILE) for k in range(tiles)]
    copies = []
    for k, span in enumerate(spans):
        tile = [pltpu.make_async_copy(s_hbm.at[span], s_ref.at[span], sems.at[k, count])]
        for h, (rows, start) in enumerate(zip(CHUNKS, STARTS)):
            there = lhs_ref.at[pl.ds(start * PEERS, rows * PEERS), span]
            tile.append(pltpu.make_async_copy(pieces[h].at[:, span], there, sems.at[k, h]))
        copies.append(tile)
    for tile in copies:
        for copy in tile:
            copy.start()
    for k, span in enumerate(spans):
        for copy in copies[k]:
            copy.wait()
        lhs = lhs_ref[:, span]
        term = jnp.dot(lhs, s_ref[span, :], preferred_element_type=jnp.float32)
        if k == 0:
            total[...] = term
        elif k < tiles - 1:
            total[...] += term
        else:
            term += total[...]
    base = 0
    for rows, start in zip(CHUNKS, STARTS):
        for peer in range(PEERS):
            slot = slot_of(z, c % 2, peer)
            out_ref[slot, start : start + rows, :] = term[base : base + rows, :]
            base += rows


def product(pieces, s_both):
    blk, cols = s_both.shape
    block_rows = sum(CHUNKS)
    hbm = pl.BlockSpec(memory_space=pltpu.HBM)
    return pl.pallas_call(
        product_kernel,
        out_shape=jax.ShapeDtypeStruct((PEERS, block_rows, cols), jnp.float32),
        in_specs=[hbm] * (len(pieces) + 1),
        out_specs=pl.BlockSpec(memory_space=pltpu.VMEM),
        scratch_shapes=[
            pltpu.VMEM((PEERS * block_rows, cols), jnp.float32),
            pltpu.VMEM((PEERS * block_rows, blk), jnp.bfloat16),
            pltpu.VMEM((blk, cols), jnp.bfloat16),
            pltpu.SemaphoreType.DMA((blk // K_TILE, len(CHUNKS) + 1)),
        ],
        compiler_params=pltpu.CompilerParams(vmem_limit_bytes=24 * 2**20),
    )(*pieces, s_both)


def col_move(value, target):
    pairs = []
    for c in range(16):
        x, y, core = c // 4, c // 2 % 2, c % 2
        tx, ty, tcore = target(x, y, core)
        pairs.append((c, tx % 4 * 4 + ty * 2 + tcore))
    return lax.ppermute(value, "col", pairs)


def slice_move(value, target):
    pairs = []
    for g in range(32):
        for c in range(16):
            to = target(g // 2, g % 2, c)
            if to is not None:
                pairs.append((g * 16 + c, (to[0] % 16 * 2 + to[1]) * 16 + to[2]))
    return lax.ppermute(value, ("grp", "col"), pairs)


def exchange(step, z, y_hi, c):
    even = (c - z) % 2 == 0
    return (z + 1 if even == (step % 2 == 1) else z - 1, y_hi, c)


def combine_kernel(*refs):
    own_ref, arrived_ref = refs[0], refs[1]
    here, sems = refs[-2:]
    handed_on = len(refs) == 8
    copies_hbm = refs[4 if handed_on else 3]
    here[...] = own_ref[...] + arrived_ref[...]
    rows = here.shape[0]
    copies = [
        pltpu.make_async_copy(here, copies_hbm.at[pl.ds(peer * rows, rows)], sems.at[peer]) for peer in range(PEERS)
    ]
    for copy in copies:
        copy.start()
    if handed_on:
        refs[5][...] = refs[2][...]
    for copy in copies:
        copy.wait()


def combine(own, arrived, following, after):
    arrays = [own, arrived] + ([] if following is None else [following])
    whole = pl.BlockSpec(memory_space=pltpu.VMEM)
    return pl.pallas_call(
        combine_kernel,
        out_shape=[jax.ShapeDtypeStruct((PEERS * own.shape[0], own.shape[1]), own.dtype)]
        + [jax.ShapeDtypeStruct(a.shape, a.dtype) for a in arrays[2:]],
        in_specs=[whole] * len(arrays) + [pl.BlockSpec(memory_space=pl.ANY)],
        out_specs=[pl.BlockSpec(memory_space=pltpu.HBM)] + [whole] * (len(arrays) - 2),
        scratch_shapes=[pltpu.VMEM(own.shape, own.dtype), pltpu.SemaphoreType.DMA((PEERS,))],
        compiler_params=pltpu.CompilerParams(vmem_limit_bytes=4 * 2**20),
    )(*arrays, after)


def add_term_kernel(slot, terms_ref, arrived_ref, after_ref, out_ref):
    out_ref[...] = terms_ref[slot] + arrived_ref[...]


def add_term(terms, slot, arrived, after):
    whole = pl.BlockSpec(memory_space=pltpu.VMEM)
    return pl.pallas_call(
        functools.partial(add_term_kernel, slot),
        out_shape=jax.ShapeDtypeStruct(arrived.shape, arrived.dtype),
        in_specs=[whole, whole, pl.BlockSpec(memory_space=pl.ANY)],
        out_specs=whole,
        compiler_params=pltpu.CompilerParams(vmem_limit_bytes=4 * 2**20),
    )(terms, arrived, after)


def gather_col(copies):
    groups = [[peer * 2 + core for peer in range(PEERS)] for core in range(2)]
    return lax.all_to_all(copies, "col", 0, 0, axis_index_groups=groups, tiled=True)


def per_device(window_rows, secular, source, kept_count):
    blk = secular.shape[0]
    g = lax.axis_index("grp")
    c = lax.axis_index("col")
    z, y_hi = g // 2, g % 2
    is_odd = (c + z) % 2 == 1
    own_base = g * blk
    partner_base = jnp.bitwise_xor(g, 16) * blk

    other = col_move(secular, lambda x, y, k: (x, y, 1 - k))
    inside = (source >= own_base) & (source < own_base + blk)
    place = jnp.where(inside, source - own_base, blk + source - partner_base)
    *parts, flag = scatter_rows(place, window_rows.T)
    own_parts, cross_parts = parts[: len(CHUNKS)], parts[len(CHUNKS) :]
    s_both, masked = split_halves(kept_count, flag, secular, other)

    pieces = []
    leaving = cross_parts[0]
    for h in range(len(CHUNKS)):
        arrived = lax.ppermute(leaving, "grp", [(i, i ^ 16) for i in range(32)])
        here, *next_leaving = combine(own_parts[h], arrived, cross_parts[h + 1] if h + 1 < len(CHUNKS) else None, masked)
        if next_leaving:
            leaving = next_leaving[0]
        pieces.append(gather_col(here))

    s_both = pltpu.with_memory_space_constraint(s_both, pltpu.HBM)
    pieces = [pltpu.with_memory_space_constraint(piece, pltpu.HBM) for piece in pieces]
    terms = product(pieces, s_both)
    outer, inner = terms[0], terms[4]
    for step in range(1, 4):
        outer = terms[step] + slice_move(outer, functools.partial(exchange, step))
        inner = slice_move(inner, functools.partial(exchange, step))
        inner = add_term(terms, 4 + step, inner, outer) if step < 3 else terms[7] + inner
    inner += slice_move(outer, lambda z, y_hi, c: (z + 4 if (c - z) % 2 else z - 4, y_hi, c))

    half_cols = inner.shape[1] // 2
    mine, theirs = inner[:, :half_cols], inner[:, half_cols:]
    rows = mine.shape[0] // 2

    def part(value, y):
        return jnp.where(y == 1, value[rows:], value[:rows])

    def odd_or_even(when_odd, when_even):
        def target(z, y_hi, c):
            is_odd = (c - z) % 2
            flips = when_odd if is_odd else when_even
            return None if flips is None else (z + is_odd, y_hi ^ flips[0], c ^ flips[1])

        return target

    mine_here, mine_across = part(mine, y_hi), part(mine, 1 - y_hi)
    theirs_here, theirs_across = part(theirs, y_hi), part(theirs, 1 - y_hi)
    total = slice_move(theirs_across, odd_or_even((1, 1), None))
    total += slice_move(jnp.where(is_odd, mine_here, theirs_here), odd_or_even((0, 0), (0, 1)))
    total += slice_move(jnp.where(is_odd, mine_across, theirs_across), odd_or_even((1, 0), (1, 1)))
    total += slice_move(jnp.where(is_odd, theirs_here, mine_across), odd_or_even((0, 1), (1, 0)))
    final = jnp.where(is_odd, total, total + mine_here).astype(jnp.bfloat16)
    return final.reshape(rows, 2, -1).transpose(1, 0, 2)


def solution(mesh):
    return jax.shard_map(
        per_device,
        mesh=mesh,
        in_specs=(P("grp", "col"), P("grp", "col"), P("grp"), P()),
        out_specs=P(None, "grp", "col"),
        check_vma=False,
    )
```

```python
import functools

import jax
import jax.numpy as jnp
from jax import lax
from jax.experimental import pallas as pl
from jax.experimental.pallas import tpu as pltpu
from jax.sharding import PartitionSpec as P

LANES = 128
UNROLL = 32
K_TILE = 768
CHUNKS = (32, 32)
STARTS = tuple(sum(CHUNKS[:h]) for h in range(len(CHUNKS)))
PEERS = 8


def scatter_kernel(place_ref, w_ref, *refs):
    outs, flag_ref, rows, spread = refs[:-3], refs[-3], refs[-2], refs[-1]
    width, blk = w_ref.shape
    ones = jnp.ones((LANES - width, LANES), jnp.float32)
    spread[...] = jnp.zeros_like(spread)
    for at in range(0, blk, LANES):
        part = w_ref[:, at : at + LANES].astype(jnp.float32)
        rows[at : at + LANES, :] = jnp.concatenate([part, ones], axis=0).T

    def move(i, carry):
        for u in range(UNROLL):
            j = i * UNROLL + u
            spread[pl.ds(place_ref[j], 1), :] = rows[pl.ds(j, 1), :]
        return carry

    lax.fori_loop(0, blk // UNROLL, move, 0)
    for side in range(2):
        for at in range(0, blk, LANES):
            block = spread[side * blk + at : side * blk + at + LANES, :]
            turned = block.T[:width].astype(jnp.bfloat16)
            for h, start in enumerate(STARTS):
                outs[side * len(CHUNKS) + h][:, at : at + LANES] = turned[start : start + CHUNKS[h]]
            if side == 0:
                mark = block[:, width:]
                flag_ref[at : at + LANES, :] = jnp.concatenate([mark, mark], axis=1).astype(jnp.bfloat16)


def scatter_rows(place, w_t):
    width, blk = w_t.shape
    return pl.pallas_call(
        scatter_kernel,
        out_shape=[jax.ShapeDtypeStruct((rows, blk), jnp.bfloat16) for rows in CHUNKS] * 2
        + [jax.ShapeDtypeStruct((blk, LANES), jnp.bfloat16)],
        in_specs=[pl.BlockSpec(memory_space=pltpu.SMEM), pl.BlockSpec(memory_space=pltpu.VMEM)],
        out_specs=[pl.BlockSpec(memory_space=pltpu.VMEM)] * (2 * len(CHUNKS) + 1),
        scratch_shapes=[pltpu.VMEM((blk, LANES), jnp.float32), pltpu.VMEM((2 * blk, LANES), jnp.float32)],
        compiler_params=pltpu.CompilerParams(vmem_limit_bytes=16 * 2**20),
    )(place, w_t)


def halves_kernel(kept_ref, flag_ref, own_ref, other_ref, out_ref, done_ref):
    tile, cols = own_ref.shape
    g = lax.axis_index("grp")
    base = (g * pl.num_programs(0) + pl.program_id(0)) * tile
    row = lax.broadcasted_iota(jnp.int32, (tile, LANES), 0) + base
    done_ref[...] = jnp.zeros_like(done_ref)
    mark = flag_ref[...].astype(jnp.float32)
    alive = row < kept_ref[0]
    mine = alive & (mark > 0.5)
    theirs = alive & (mark < 0.5)
    lower = g >= 16
    in_half = (
        jnp.where(lower, theirs.astype(jnp.float32), mine.astype(jnp.float32)),
        jnp.where(lower, mine.astype(jnp.float32), theirs.astype(jnp.float32)),
    )
    for c, ref in enumerate((own_ref, other_ref)):
        for h in range(2):
            for v in range(cols // LANES):
                values = ref[:, v * LANES : (v + 1) * LANES].astype(jnp.float32)
                at = (c * 2 + h) * cols + v * LANES
                out_ref[:, at : at + LANES] = jnp.where(in_half[h] > 0.5, values, 0.0).astype(jnp.bfloat16)


def split_halves(kept, flag, own, other):
    blk, cols = own.shape
    return pl.pallas_call(
        halves_kernel,
        grid=(blk // K_TILE,),
        out_shape=[
            jax.ShapeDtypeStruct((blk, 4 * cols), jnp.bfloat16),
            jax.ShapeDtypeStruct((8, LANES), jnp.float32),
        ],
        in_specs=[
            pl.BlockSpec(memory_space=pltpu.SMEM),
            pl.BlockSpec((K_TILE, LANES), lambda i: (i, 0)),
            pl.BlockSpec((K_TILE, cols), lambda i: (i, 0)),
            pl.BlockSpec((K_TILE, cols), lambda i: (i, 0)),
        ],
        out_specs=[pl.BlockSpec((K_TILE, 4 * cols), lambda i: (i, 0)), pl.BlockSpec((8, LANES), lambda i: (0, 0))],
        compiler_params=pltpu.CompilerParams(vmem_limit_bytes=12 * 2**20),
    )(kept, flag, own, other)


def slot_of(z, core, peer):
    odd = (core + z) % 2
    target = peer * 2 + core
    above = (target + 16 - z - odd) % 16 // 2
    even_slot = jnp.where(above > 4, 2 * above - 9, jnp.minimum(8 - 2 * above, 7))
    odd_slot = jnp.where(above > 4, 2 * above - 8, jnp.maximum(7 - 2 * above, 0))
    return jnp.where(odd == 1, odd_slot, even_slot)


def product_kernel(piece_hbm, s_hbm, *refs):
    out_ref, total, lhs_ref, s_ref, sems = refs[-5:]
    z, c = lax.axis_index("grp") // 2, lax.axis_index("col")
    tiles = s_ref.shape[0] // K_TILE
    spans = [pl.ds(k * K_TILE, K_TILE) for k in range(tiles)]
    copies = [
        (
            pltpu.make_async_copy(s_hbm.at[span], s_ref.at[span], sems.at[k, 0]),
            pltpu.make_async_copy(piece_hbm.at[:, span], lhs_ref.at[:, span], sems.at[k, 1]),
        )
        for k, span in enumerate(spans)
    ]
    for tile in copies:
        for copy in tile:
            copy.start()
    for k, span in enumerate(spans):
        for copy in copies[k]:
            copy.wait()
        term = jnp.dot(lhs_ref[:, span], s_ref[span, :], preferred_element_type=jnp.float32)
        if k == 0:
            total[...] = term
        elif k < tiles - 1:
            total[...] += term
        else:
            term += total[...]
    rows = out_ref.shape[1]
    for peer in range(PEERS):
        out_ref[slot_of(z, c % 2, peer)] = term[peer * rows : (peer + 1) * rows, :]


def product(piece, s_both, after):
    blk, cols = s_both.shape
    rows = piece.shape[0]
    return pl.pallas_call(
        product_kernel,
        out_shape=jax.ShapeDtypeStruct((PEERS, rows // PEERS, cols), jnp.float32),
        in_specs=[pl.BlockSpec(memory_space=pltpu.HBM)] * 2 + [pl.BlockSpec(memory_space=pl.ANY)] * len(after),
        out_specs=pl.BlockSpec(memory_space=pltpu.VMEM),
        scratch_shapes=[
            pltpu.VMEM((rows, cols), jnp.float32),
            pltpu.VMEM((rows, blk), jnp.bfloat16),
            pltpu.VMEM((blk, cols), jnp.bfloat16),
            pltpu.SemaphoreType.DMA((blk // K_TILE, 2)),
        ],
        compiler_params=pltpu.CompilerParams(vmem_limit_bytes=20 * 2**20),
    )(pltpu.with_memory_space_constraint(piece, pltpu.HBM), s_both, *after)


def col_move(value, target):
    pairs = []
    for c in range(16):
        x, y, core = c // 4, c // 2 % 2, c % 2
        tx, ty, tcore = target(x, y, core)
        pairs.append((c, tx % 4 * 4 + ty * 2 + tcore))
    return lax.ppermute(value, "col", pairs)


def slice_move(value, target):
    pairs = []
    for g in range(32):
        for c in range(16):
            to = target(g // 2, g % 2, c)
            if to is not None:
                pairs.append((g * 16 + c, (to[0] % 16 * 2 + to[1]) * 16 + to[2]))
    return lax.ppermute(value, ("grp", "col"), pairs)


def exchange(step, z, y_hi, c):
    even = (c - z) % 2 == 0
    return (z + 1 if even == (step % 2 == 1) else z - 1, y_hi, c)


def combine_kernel(*refs):
    own_ref, arrived_ref = refs[0], refs[1]
    here, sems = refs[-2:]
    handed_on = len(refs) == 8
    copies_hbm = refs[4 if handed_on else 3]
    here[...] = own_ref[...] + arrived_ref[...]
    rows = here.shape[0]
    copies = [
        pltpu.make_async_copy(here, copies_hbm.at[pl.ds(peer * rows, rows)], sems.at[peer]) for peer in range(PEERS)
    ]
    for copy in copies:
        copy.start()
    if handed_on:
        refs[5][...] = refs[2][...]
    for copy in copies:
        copy.wait()


def combine(own, arrived, following, after):
    arrays = [own, arrived] + ([] if following is None else [following])
    whole = pl.BlockSpec(memory_space=pltpu.VMEM)
    return pl.pallas_call(
        combine_kernel,
        out_shape=[jax.ShapeDtypeStruct((PEERS * own.shape[0], own.shape[1]), own.dtype)]
        + [jax.ShapeDtypeStruct(a.shape, a.dtype) for a in arrays[2:]],
        in_specs=[whole] * len(arrays) + [pl.BlockSpec(memory_space=pl.ANY)],
        out_specs=[pl.BlockSpec(memory_space=pltpu.HBM)] + [whole] * (len(arrays) - 2),
        scratch_shapes=[pltpu.VMEM(own.shape, own.dtype), pltpu.SemaphoreType.DMA((PEERS,))],
        compiler_params=pltpu.CompilerParams(vmem_limit_bytes=4 * 2**20),
    )(*arrays, after)


def add_term_kernel(slot, terms_ref, arrived_ref, after_ref, out_ref):
    out_ref[...] = terms_ref[slot] + arrived_ref[...]


def add_term(terms, slot, arrived, after):
    whole = pl.BlockSpec(memory_space=pltpu.VMEM)
    return pl.pallas_call(
        functools.partial(add_term_kernel, slot),
        out_shape=jax.ShapeDtypeStruct(arrived.shape, arrived.dtype),
        in_specs=[whole, whole, pl.BlockSpec(memory_space=pl.ANY)],
        out_specs=whole,
        compiler_params=pltpu.CompilerParams(vmem_limit_bytes=4 * 2**20),
    )(terms, arrived, after)


def gather_col(copies):
    groups = [[peer * 2 + core for peer in range(PEERS)] for core in range(2)]
    return lax.all_to_all(copies, "col", 0, 0, axis_index_groups=groups, tiled=True)


def sum_near(terms):
    outer, inner = terms[0], terms[4]
    for step in range(1, 4):
        outer = terms[step] + slice_move(outer, functools.partial(exchange, step))
        inner = slice_move(inner, functools.partial(exchange, step))
        if step < 3:
            inner = near = add_term(terms, 4 + step, inner, outer)
        else:
            inner = terms[7] + inner
    inner += slice_move(outer, lambda z, y_hi, c: (z + 4 if (c - z) % 2 else z - 4, y_hi, c))
    return inner, [outer, near]


def per_device(window_rows, secular, source, kept_count):
    blk = secular.shape[0]
    g = lax.axis_index("grp")
    c = lax.axis_index("col")
    z, y_hi = g // 2, g % 2
    is_odd = (c + z) % 2 == 1
    own_base = g * blk
    partner_base = jnp.bitwise_xor(g, 16) * blk

    other = col_move(secular, lambda x, y, k: (x, y, 1 - k))
    inside = (source >= own_base) & (source < own_base + blk)
    place = jnp.where(inside, source - own_base, blk + source - partner_base)
    *parts, flag = scatter_rows(place, window_rows.T)
    own_parts, cross_parts = parts[: len(CHUNKS)], parts[len(CHUNKS) :]
    s_both, masked = split_halves(kept_count, flag, secular, other)

    pieces = []
    leaving = cross_parts[0]
    for h in range(len(CHUNKS)):
        arrived = lax.ppermute(leaving, "grp", [(i, i ^ 16) for i in range(32)])
        here, *next_leaving = combine(own_parts[h], arrived, cross_parts[h + 1] if h + 1 < len(CHUNKS) else None, masked)
        if next_leaving:
            leaving = next_leaving[0]
        pieces.append(gather_col(here))

    s_both = pltpu.with_memory_space_constraint(s_both, pltpu.HBM)
    sums, after = [], [masked]
    for piece in pieces:
        total, after = sum_near(product(piece, s_both, after))
        sums.append(total)
    inner = jnp.concatenate(sums, axis=0)

    half_cols = inner.shape[1] // 2
    mine, theirs = inner[:, :half_cols], inner[:, half_cols:]
    rows = mine.shape[0] // 2

    def part(value, y):
        return jnp.where(y == 1, value[rows:], value[:rows])

    def odd_or_even(when_odd, when_even):
        def target(z, y_hi, c):
            is_odd = (c - z) % 2
            flips = when_odd if is_odd else when_even
            return None if flips is None else (z + is_odd, y_hi ^ flips[0], c ^ flips[1])

        return target

    mine_here, mine_across = part(mine, y_hi), part(mine, 1 - y_hi)
    theirs_here, theirs_across = part(theirs, y_hi), part(theirs, 1 - y_hi)
    total = slice_move(theirs_across, odd_or_even((1, 1), None))
    total += slice_move(jnp.where(is_odd, mine_here, theirs_here), odd_or_even((0, 0), (0, 1)))
    total += slice_move(jnp.where(is_odd, mine_across, theirs_across), odd_or_even((1, 0), (1, 1)))
    total += slice_move(jnp.where(is_odd, theirs_here, mine_across), odd_or_even((0, 1), (1, 0)))
    final = jnp.where(is_odd, total, total + mine_here).astype(jnp.bfloat16)
    return final.reshape(rows, 2, -1).transpose(1, 0, 2)


def solution(mesh):
    return jax.shard_map(
        per_device,
        mesh=mesh,
        in_specs=(P("grp", "col"), P("grp", "col"), P("grp"), P()),
        out_specs=P(None, "grp", "col"),
        check_vma=False,
    )
```

```python
import functools

import jax
import jax.numpy as jnp
from jax import lax
from jax.experimental import pallas as pl
from jax.experimental.pallas import tpu as pltpu
from jax.sharding import PartitionSpec as P

LANES = 128
UNROLL = 32
K_TILE = 768
CHUNKS = (32, 32)
STARTS = tuple(sum(CHUNKS[:h]) for h in range(len(CHUNKS)))
PEERS = 8


def scatter_kernel(place_ref, w_ref, *refs):
    outs, flag_ref, rows, spread = refs[:-3], refs[-3], refs[-2], refs[-1]
    width, blk = w_ref.shape
    ones = jnp.ones((LANES - width, LANES), jnp.float32)
    spread[...] = jnp.zeros_like(spread)
    for at in range(0, blk, LANES):
        part = w_ref[:, at : at + LANES].astype(jnp.float32)
        rows[at : at + LANES, :] = jnp.concatenate([part, ones], axis=0).T

    def move(i, carry):
        for u in range(UNROLL):
            j = i * UNROLL + u
            spread[pl.ds(place_ref[j], 1), :] = rows[pl.ds(j, 1), :]
        return carry

    lax.fori_loop(0, blk // UNROLL, move, 0)
    for side in range(2):
        for at in range(0, blk, LANES):
            block = spread[side * blk + at : side * blk + at + LANES, :]
            turned = block.T[:width].astype(jnp.bfloat16)
            for h, start in enumerate(STARTS):
                outs[side * len(CHUNKS) + h][:, at : at + LANES] = turned[start : start + CHUNKS[h]]
            if side == 0:
                mark = block[:, width:]
                flag_ref[at : at + LANES, :] = jnp.concatenate([mark, mark], axis=1).astype(jnp.bfloat16)


def scatter_rows(place, w_t):
    width, blk = w_t.shape
    return pl.pallas_call(
        scatter_kernel,
        out_shape=[jax.ShapeDtypeStruct((rows, blk), jnp.bfloat16) for rows in CHUNKS] * 2
        + [jax.ShapeDtypeStruct((blk, LANES), jnp.bfloat16)],
        in_specs=[pl.BlockSpec(memory_space=pltpu.SMEM), pl.BlockSpec(memory_space=pltpu.VMEM)],
        out_specs=[pl.BlockSpec(memory_space=pltpu.VMEM)] * (2 * len(CHUNKS) + 1),
        scratch_shapes=[pltpu.VMEM((blk, LANES), jnp.float32), pltpu.VMEM((2 * blk, LANES), jnp.float32)],
        compiler_params=pltpu.CompilerParams(vmem_limit_bytes=16 * 2**20),
    )(place, w_t)


def halves_kernel(kept_ref, flag_ref, own_ref, other_ref, out_ref, done_ref):
    tile, cols = own_ref.shape
    g = lax.axis_index("grp")
    base = (g * pl.num_programs(0) + pl.program_id(0)) * tile
    row = lax.broadcasted_iota(jnp.int32, (tile, LANES), 0) + base
    done_ref[...] = jnp.zeros_like(done_ref)
    mark = flag_ref[...].astype(jnp.float32)
    alive = row < kept_ref[0]
    mine = alive & (mark > 0.5)
    theirs = alive & (mark < 0.5)
    lower = g >= 16
    in_half = (
        jnp.where(lower, theirs.astype(jnp.float32), mine.astype(jnp.float32)),
        jnp.where(lower, mine.astype(jnp.float32), theirs.astype(jnp.float32)),
    )
    for c, ref in enumerate((own_ref, other_ref)):
        for h in range(2):
            for v in range(cols // LANES):
                values = ref[:, v * LANES : (v + 1) * LANES].astype(jnp.float32)
                at = (c * 2 + h) * cols + v * LANES
                out_ref[:, at : at + LANES] = jnp.where(in_half[h] > 0.5, values, 0.0).astype(jnp.bfloat16)


def split_halves(kept, flag, own, other):
    blk, cols = own.shape
    return pl.pallas_call(
        halves_kernel,
        grid=(blk // K_TILE,),
        out_shape=[
            jax.ShapeDtypeStruct((blk, 4 * cols), jnp.bfloat16),
            jax.ShapeDtypeStruct((8, LANES), jnp.float32),
        ],
        in_specs=[
            pl.BlockSpec(memory_space=pltpu.SMEM),
            pl.BlockSpec((K_TILE, LANES), lambda i: (i, 0)),
            pl.BlockSpec((K_TILE, cols), lambda i: (i, 0)),
            pl.BlockSpec((K_TILE, cols), lambda i: (i, 0)),
        ],
        out_specs=[pl.BlockSpec((K_TILE, 4 * cols), lambda i: (i, 0)), pl.BlockSpec((8, LANES), lambda i: (0, 0))],
        compiler_params=pltpu.CompilerParams(vmem_limit_bytes=12 * 2**20),
    )(kept, flag, own, other)


def slot_of(z, core, peer):
    odd = (core + z) % 2
    target = peer * 2 + core
    above = (target + 16 - z - odd) % 16 // 2
    even_slot = jnp.where(above > 4, 2 * above - 9, jnp.minimum(8 - 2 * above, 7))
    odd_slot = jnp.where(above > 4, 2 * above - 8, jnp.maximum(7 - 2 * above, 0))
    return jnp.where(odd == 1, odd_slot, even_slot)


def product_kernel(piece_hbm, s_hbm, *refs):
    out_ref, total, lhs_ref, s_ref, sems = refs[-5:]
    z, c = lax.axis_index("grp") // 2, lax.axis_index("col")
    tiles = s_ref.shape[0] // K_TILE
    spans = [pl.ds(k * K_TILE, K_TILE) for k in range(tiles)]
    copies = [
        (
            pltpu.make_async_copy(s_hbm.at[span], s_ref.at[span], sems.at[k, 0]),
            pltpu.make_async_copy(piece_hbm.at[:, span], lhs_ref.at[:, span], sems.at[k, 1]),
        )
        for k, span in enumerate(spans)
    ]
    for tile in copies:
        for copy in tile:
            copy.start()
    for k, span in enumerate(spans):
        for copy in copies[k]:
            copy.wait()
        term = jnp.dot(lhs_ref[:, span], s_ref[span, :], preferred_element_type=jnp.float32)
        if k == 0:
            total[...] = term
        elif k < tiles - 1:
            total[...] += term
        else:
            term += total[...]
    rows = out_ref.shape[1]
    for peer in range(PEERS):
        out_ref[slot_of(z, c % 2, peer)] = term[peer * rows : (peer + 1) * rows, :]


def product(piece, s_both, after):
    blk, cols = s_both.shape
    rows = piece.shape[0]
    return pl.pallas_call(
        product_kernel,
        out_shape=jax.ShapeDtypeStruct((PEERS, rows // PEERS, cols), jnp.float32),
        in_specs=[pl.BlockSpec(memory_space=pltpu.HBM)] * 2 + [pl.BlockSpec(memory_space=pl.ANY)] * len(after),
        out_specs=pl.BlockSpec(memory_space=pltpu.VMEM),
        scratch_shapes=[
            pltpu.VMEM((rows, cols), jnp.float32),
            pltpu.VMEM((rows, blk), jnp.bfloat16),
            pltpu.VMEM((blk, cols), jnp.bfloat16),
            pltpu.SemaphoreType.DMA((blk // K_TILE, 2)),
        ],
        compiler_params=pltpu.CompilerParams(vmem_limit_bytes=20 * 2**20),
    )(pltpu.with_memory_space_constraint(piece, pltpu.HBM), s_both, *after)


def col_move(value, target):
    pairs = []
    for c in range(16):
        x, y, core = c // 4, c // 2 % 2, c % 2
        tx, ty, tcore = target(x, y, core)
        pairs.append((c, tx % 4 * 4 + ty * 2 + tcore))
    return lax.ppermute(value, "col", pairs)


def slice_move(value, target):
    pairs = []
    for g in range(32):
        for c in range(16):
            to = target(g // 2, g % 2, c)
            if to is not None:
                pairs.append((g * 16 + c, (to[0] % 16 * 2 + to[1]) * 16 + to[2]))
    return lax.ppermute(value, ("grp", "col"), pairs)


def exchange(step, z, y_hi, c):
    even = (c - z) % 2 == 0
    return (z + 1 if even == (step % 2 == 1) else z - 1, y_hi, c)


def combine_kernel(*refs):
    own_ref, arrived_ref = refs[0], refs[1]
    here, sems = refs[-2:]
    handed_on = len(refs) == 8
    copies_hbm = refs[4 if handed_on else 3]
    here[...] = own_ref[...] + arrived_ref[...]
    rows = here.shape[0]
    copies = [
        pltpu.make_async_copy(here, copies_hbm.at[pl.ds(peer * rows, rows)], sems.at[peer]) for peer in range(PEERS)
    ]
    for copy in copies:
        copy.start()
    if handed_on:
        refs[5][...] = refs[2][...]
    for copy in copies:
        copy.wait()


def combine(own, arrived, following, after):
    arrays = [own, arrived] + ([] if following is None else [following])
    whole = pl.BlockSpec(memory_space=pltpu.VMEM)
    return pl.pallas_call(
        combine_kernel,
        out_shape=[jax.ShapeDtypeStruct((PEERS * own.shape[0], own.shape[1]), own.dtype)]
        + [jax.ShapeDtypeStruct(a.shape, a.dtype) for a in arrays[2:]],
        in_specs=[whole] * len(arrays) + [pl.BlockSpec(memory_space=pl.ANY)],
        out_specs=[pl.BlockSpec(memory_space=pltpu.HBM)] + [whole] * (len(arrays) - 2),
        scratch_shapes=[pltpu.VMEM(own.shape, own.dtype), pltpu.SemaphoreType.DMA((PEERS,))],
        compiler_params=pltpu.CompilerParams(vmem_limit_bytes=4 * 2**20),
    )(*arrays, after)


def add_term_kernel(slot, terms_ref, arrived_ref, *refs):
    refs[-1][...] = terms_ref[slot] + arrived_ref[...]


def add_term(terms, slot, arrived, *after):
    whole = pl.BlockSpec(memory_space=pltpu.VMEM)
    return pl.pallas_call(
        functools.partial(add_term_kernel, slot),
        out_shape=jax.ShapeDtypeStruct(arrived.shape, arrived.dtype),
        in_specs=[whole, whole] + [pl.BlockSpec(memory_space=pl.ANY)] * len(after),
        out_specs=whole,
        compiler_params=pltpu.CompilerParams(vmem_limit_bytes=4 * 2**20),
    )(terms, arrived, *after)


def gather_col(copies):
    groups = [[peer * 2 + core for peer in range(PEERS)] for core in range(2)]
    return lax.all_to_all(copies, "col", 0, 0, axis_index_groups=groups, tiled=True)


def sum_near(terms, before):
    outer, inner = terms[0], terms[4]
    for step in range(1, 4):
        outer = terms[step] + slice_move(outer, functools.partial(exchange, step))
        inner = slice_move(inner, functools.partial(exchange, step))
        if step < 3:
            inner = add_term(terms, 4 + step, inner, outer, *(before if step == 1 else []))
    inner = add_term(terms, 7, inner)
    skipped = slice_move(outer, lambda z, y_hi, c: (z + 4 if (c - z) % 2 else z - 4, y_hi, c))
    return inner, skipped, outer


def per_device(window_rows, secular, source, kept_count):
    blk = secular.shape[0]
    g = lax.axis_index("grp")
    c = lax.axis_index("col")
    z, y_hi = g // 2, g % 2
    is_odd = (c + z) % 2 == 1
    own_base = g * blk
    partner_base = jnp.bitwise_xor(g, 16) * blk

    other = col_move(secular, lambda x, y, k: (x, y, 1 - k))
    inside = (source >= own_base) & (source < own_base + blk)
    place = jnp.where(inside, source - own_base, blk + source - partner_base)
    *parts, flag = scatter_rows(place, window_rows.T)
    own_parts, cross_parts = parts[: len(CHUNKS)], parts[len(CHUNKS) :]
    s_both, masked = split_halves(kept_count, flag, secular, other)

    pieces = []
    leaving = cross_parts[0]
    for h in range(len(CHUNKS)):
        arrived = lax.ppermute(leaving, "grp", [(i, i ^ 16) for i in range(32)])
        here, *next_leaving = combine(own_parts[h], arrived, cross_parts[h + 1] if h + 1 < len(CHUNKS) else None, masked)
        if next_leaving:
            leaving = next_leaving[0]
        pieces.append(gather_col(here))

    s_both = pltpu.with_memory_space_constraint(s_both, pltpu.HBM)
    sums, after, before = [], [masked], []
    for piece in pieces:
        inner, skipped, outer = sum_near(product(piece, s_both, after), before)
        sums.append(inner + skipped)
        after, before = [outer, inner], [skipped]
    inner = jnp.concatenate(sums, axis=0)

    half_cols = inner.shape[1] // 2
    mine, theirs = inner[:, :half_cols], inner[:, half_cols:]
    rows = mine.shape[0] // 2

    def part(value, y):
        return jnp.where(y == 1, value[rows:], value[:rows])

    def odd_or_even(when_odd, when_even):
        def target(z, y_hi, c):
            is_odd = (c - z) % 2
            flips = when_odd if is_odd else when_even
            return None if flips is None else (z + is_odd, y_hi ^ flips[0], c ^ flips[1])

        return target

    mine_here, mine_across = part(mine, y_hi), part(mine, 1 - y_hi)
    theirs_here, theirs_across = part(theirs, y_hi), part(theirs, 1 - y_hi)
    total = slice_move(theirs_across, odd_or_even((1, 1), None))
    total += slice_move(jnp.where(is_odd, mine_here, theirs_here), odd_or_even((0, 0), (0, 1)))
    total += slice_move(jnp.where(is_odd, mine_across, theirs_across), odd_or_even((1, 0), (1, 1)))
    total += slice_move(jnp.where(is_odd, theirs_here, mine_across), odd_or_even((0, 1), (1, 0)))
    final = jnp.where(is_odd, total, total + mine_here).astype(jnp.bfloat16)
    return final.reshape(rows, 2, -1).transpose(1, 0, 2)


def solution(mesh):
    return jax.shard_map(
        per_device,
        mesh=mesh,
        in_specs=(P("grp", "col"), P("grp", "col"), P("grp"), P()),
        out_specs=P(None, "grp", "col"),
        check_vma=False,
    )
```
